512 devices in a mesh: wide: 64 (over z, y), ply: 8 (over x, core).
Axes of the slice: x: 4, y: 4, z: 16, core: 2. Of those that a mesh axis runs over, the one named last changes fastest.
Arguments:
- interior_inverse: bfloat16 [1536, 640, 640], P(('wide', 'ply')), may hold values from -0.25 to 0.25
- coupling: bfloat16 [1536, 640, 512], P(('wide', 'ply')), may hold values from -0.83984375 to 0.83984375
- boundary_stiffness: bfloat16 [1536, 512], P(('wide', 'ply')), may hold values from 1 to 10
- interior_load: bfloat16 [1536, 640], P(('wide', 'ply')), may hold values from -6 to 6
- boundary_load: bfloat16 [1536, 512], P(('wide', 'ply')), may hold values from -6 to 6
- touch_ply: int32 [6144, 1], P(('wide', 'ply')), may hold values from 0 to 7; in each aligned block of 12 rows (0 to 11, 12 to 23, ...) at most 3 rows name the same one
- touch_slot: int32 [6144], P(('wide', 'ply')), may hold values from 0 to 3
- source_position: int32 [8, 256], P('ply'), may hold values from 0 to 255, each once within a row
Outputs:
- interface_blocks: float32 [8, 128, 256, 128], P('ply', 'wide')
- interface_loads: float32 [8, 128, 256], P('ply', 'wide')
The draws below stay inside these ranges and needn't reach their ends.
Inputs may be any that keep to these rules, and one draw needn't show every extreme that they name: `touch_ply`: among the items of one device, at most 3 have the same ply index, and some device reaches 3. `source_position`: each row holds every owner position once.
All inputs are finite; a program needn't handle non-finite values.
Results may differ from the reference program's by a relative error of at most 0.004.
Values may be sent and summed in bfloat16 or wider, within the bound.
No kernel may reach another device: no remote copies, remote signals or barrier semaphores. Data moves between devices by JAX's collectives and lax.ppermute only.
A program may use at most 64 MiB of HBM per device.

```python
import math
import jax
import jax.numpy as jnp
import numpy as np
from jax import lax

NI = 640
PR = 128
NPS = 4
NB = 512
P_OWN = 4
ITEMS_DEV = 12
CAP = 3
SUBS = 1536
ITEMS = 6144
PATCHES = 256
N_PLY = 8


def place_ends(values, own_key, smallest, top_value):
    index_at = [jax.random.randint(jax.random.fold_in(own_key, axis), (), 0, length) for axis, length in enumerate(values.shape)]
    widest = values.shape.index(max(values.shape))
    next_to = index_at[:widest] + [(index_at[widest] + 1) % values.shape[widest]] + index_at[widest + 1:]
    return values.at[tuple(index_at)].set(smallest).at[tuple(next_to)].set(top_value)


def levels(rng, extent, split, smallest, largest):
    level = 1.0
    for position, blocks in split:
        steps = jax.random.uniform(jax.random.fold_in(jax.random.fold_in(rng, 6), position), (blocks,), jnp.float32, smallest / len(split), largest / len(split))
        level = level * jnp.repeat(jnp.exp(steps), extent[position] // blocks).reshape((-1,) + (1,) * (len(extent) - 1 - position))
    return level


def deal_out(key, own, number, rows, amount, top, reach, lean):
    sequence = jax.random.permutation(key, amount)
    crowded, usual = shares(amount, rows * top, reach, lean, True), shares(amount, rows * top, reach, lean, False)
    places = jnp.arange(amount)

    def named(lengths, rotation):
        used = int((lengths > 0).sum())
        fixed = max(1, used // 4)
        moved = fixed + (places - fixed + rotation * (used - fixed)) % max(1, amount - fixed)
        return jnp.zeros((amount,), jnp.int32).at[sequence[jnp.where(places < fixed, places, moved)]].set(jnp.asarray(lengths, jnp.int32))

    lengths = jnp.where(number % 4 == 0, named(crowded, number // 4), named(usual, number - number // 4 - 1))
    mixed = jax.random.permutation(jax.random.fold_in(own, 3), amount)
    source_of, receiver = mixed[0:amount // 2 * 2:2], mixed[1:amount // 2 * 2:2]
    slack = jnp.minimum(lengths[source_of] - 1, reach - lengths[receiver]) // 2
    slack = jnp.where((source_of == sequence[0]) | (receiver == sequence[0]) | (lengths[receiver] == 0), 0, jnp.maximum(slack, 0))
    moved = jax.random.randint(jax.random.fold_in(own, 4), (amount // 2,), 0, 1 << 20) % (slack + 1)
    lengths = lengths.at[source_of].add(-moved).at[receiver].add(moved)
    members = jnp.searchsorted(jnp.cumsum(lengths), jnp.arange(rows * top), side="right").astype(jnp.int32)
    grid = members.reshape(top, rows).T
    grid = grid[jax.random.permutation(jax.random.fold_in(own, 1), rows)]
    rotation = jax.random.randint(jax.random.fold_in(own, 2), (rows, 1), 0, top)
    return jnp.take_along_axis(grid, (jnp.arange(top)[None, :] + rotation) % top, axis=1)


def shares(count, total, most, skew, full):
    portions = [(1 << 20) // math.isqrt(standing ** skew) + 1 for standing in range(1, count + 1)]
    largest = most if full else min(most, max(-(-total // count), total * portions[0] // sum(portions)))
    least = 1 if total - largest >= count - 1 else 0
    counts, rest = [largest] + [least] * (count - 1), total - largest - least * (count - 1)
    while rest > 0:
        free = [i for i in range(1, count) if counts[i] < largest] or [i for i in range(1, count) if counts[i] < most]
        whole, budget = sum([portions[i] for i in free]), rest
        for i in free:
            extra = min(most - counts[i], max(1, budget * portions[i] // whole), rest)
            counts[i] = counts[i] + extra
            rest = rest - extra
    return np.array(counts)


def normal_values(rng, dims, spread, reach, split=(), kind=jnp.bfloat16):
    values = spread * jax.random.normal(rng, dims, jnp.float32)
    if split:
        values = values * levels(rng, dims, split, -0.22, 0.18)
    return jnp.clip(values, -reach, reach).astype(kind)


def setup_inputs(seed: int = 0) -> dict:
    arg_keys = jax.random.split(jax.random.key(seed), 9)
    interior_inverse = normal_values(arg_keys[0], (SUBS, NI, NI), NI ** -0.5, 0.25, ((0, 512),))
    coupling = normal_values(arg_keys[1], (SUBS, NI, NB), 0.14, 0.83984375, ((0, 512),))
    boundary_stiffness = jnp.clip(jnp.exp(math.log(10.0) - 2.3025851 * jax.random.uniform(arg_keys[2], (SUBS, NB), jnp.float32) ** levels(arg_keys[2], (SUBS, NB), ((0, 512),), -0.2, 0.2)), 1.0, 10.0).astype(jnp.bfloat16)
    interior_load = normal_values(arg_keys[3], (SUBS, NI), 1.0, 6.0, ((0, 512),))
    boundary_load = normal_values(arg_keys[4], (SUBS, NB), 1.0, 6.0, ((0, 512),))
    touch_ply_keys = jax.random.split(jax.random.fold_in(arg_keys[5], 1), ITEMS // ITEMS_DEV)
    touch_ply_turns = jax.random.permutation(jax.random.fold_in(arg_keys[5], 3), ITEMS // ITEMS_DEV)
    touch_ply = jax.vmap(lambda own, number: deal_out(jax.random.fold_in(arg_keys[5], 2), own, number, ITEMS_DEV, N_PLY, 1, CAP, 2))(touch_ply_keys, touch_ply_turns).reshape((ITEMS, 1))
    touch_slot = place_ends(jax.random.randint(arg_keys[6], (ITEMS,), 0, P_OWN), jax.random.fold_in(arg_keys[6], 1), 0, P_OWN - 1).astype(jnp.int32)
    source_position = jax.vmap(lambda own: jax.random.permutation(own, PATCHES))(jax.random.split(arg_keys[7], N_PLY)).reshape((N_PLY, PATCHES)).astype(jnp.int32)
    return dict(interior_inverse=interior_inverse, coupling=coupling, boundary_stiffness=boundary_stiffness, interior_load=interior_load, boundary_load=boundary_load, touch_ply=touch_ply, touch_slot=touch_slot, source_position=source_position)


def condense(inverse_one, coupling_one, stiffness_one, interior_one, boundary_one):
    inner_solve = jnp.dot(inverse_one, coupling_one, preferred_element_type=jnp.float32).astype(jnp.bfloat16)
    solved = jnp.dot(inverse_one, interior_one, preferred_element_type=jnp.float32).astype(jnp.bfloat16)
    split_coupling = coupling_one.astype(jnp.float32).reshape(NI, NPS, PR)
    split_inner = inner_solve.astype(jnp.float32).reshape(NI, NPS, PR)
    product = jnp.einsum('mka,mkc->kac', split_coupling, split_inner)
    identity = jnp.eye(PR, dtype=jnp.float32)
    diagonal_part = stiffness_one.astype(jnp.float32).reshape(NPS, PR)[:, :, None] * identity
    panels = (diagonal_part - product).astype(jnp.bfloat16)
    carried = jnp.dot(solved, coupling_one, preferred_element_type=jnp.float32)
    condensed = (boundary_one.astype(jnp.float32) - carried).astype(jnp.bfloat16).reshape(NPS, PR)
    return panels, condensed


def reference(interior_inverse, coupling, boundary_stiffness, interior_load, boundary_load, touch_ply, touch_slot, source_position):
    panels, condensed = lax.map(lambda group: condense(*group), (interior_inverse, coupling, boundary_stiffness, interior_load, boundary_load))
    panels = panels.reshape(ITEMS, PR, PR)
    condensed = condensed.reshape(ITEMS, PR)
    item_wide = (jnp.arange(ITEMS, dtype=jnp.int32) // ITEMS_DEV) // N_PLY
    owner = (item_wide * P_OWN + touch_slot).astype(jnp.int32)
    segment = (touch_ply[:, 0] * PATCHES + owner).astype(jnp.int32)
    owner_blocks = jax.ops.segment_sum(panels.astype(jnp.float32), segment, num_segments=N_PLY * PATCHES)
    owner_loads = jax.ops.segment_sum(condensed.astype(jnp.float32), segment, num_segments=N_PLY * PATCHES)
    owner_blocks = owner_blocks.reshape(N_PLY, PATCHES, PR, PR)
    owner_loads = owner_loads.reshape(N_PLY, PATCHES, PR)
    picked_blocks = jax.vmap(lambda table, where: table[where])(owner_blocks, source_position)
    picked_loads = jax.vmap(lambda table, where: table[where])(owner_loads, source_position)
    return jnp.transpose(picked_blocks, (0, 2, 1, 3)), jnp.transpose(picked_loads, (0, 2, 1))
```

```python
import functools

import jax
import jax.numpy as jnp
from jax import lax
from jax.experimental import pallas as pl
from jax.experimental.pallas import tpu as pltpu
from jax.sharding import PartitionSpec as P

PR = 128
NPS = 4
P_OWN = 4
CAP = 3
N_Z = 16
N_Y = 4
BITS = 2
SHARE = N_Z * BITS
CHUNK = CAP * SHARE + 8
CODE_ROW = CAP
LOADS = SHARE * P_OWN
BACK = N_Y * P_OWN * BITS + 8
VMEM_LIMIT = 40 * 1024 * 1024


def iota(shape, axis):
    return lax.broadcasted_iota(jnp.int32, shape, axis)


def condense_kernel(
    ply_ref,
    slot_ref,
    inverse_hbm,
    coupling_hbm,
    stiffness_ref,
    interior_ref,
    boundary_ref,
    out_ref,
    inverse_buf,
    coupling_buf,
    extra,
    count,
    sems,
):
    subs, inner_size, width = coupling_buf.shape
    plies = extra.shape[0]
    copies = []
    for s in range(subs):
        pair = (
            pltpu.make_async_copy(inverse_hbm.at[s], inverse_buf.at[s], sems.at[0, s]),
            pltpu.make_async_copy(coupling_hbm.at[s], coupling_buf.at[s], sems.at[1, s]),
        )
        for copy in pair:
            copy.start()
        copies.append(pair)
    out_ref[...] = jnp.zeros_like(out_ref)
    extra[...] = jnp.where(iota(extra.shape, 1) == CODE_ROW, -1.0, 0.0)
    for q in range(plies):
        count[q] = 0
    lane = iota((1, PR), 1)
    row_code = (lane % N_Z) * (BITS * P_OWN) + ((lane // N_Z) % BITS) * P_OWN
    row_item = lane // SHARE
    same = iota((PR, PR), 0) == iota((PR, PR), 1)
    row = iota((PR, PR), 0)
    source = (row % N_Z) * (N_Y * BITS) + (row // SHARE) * BITS + (row // N_Z) % BITS
    order = (source == iota((PR, PR), 1)).astype(jnp.bfloat16)
    stiffness = stiffness_ref[...].astype(jnp.float32)
    interior = interior_ref[...].astype(jnp.float32)
    boundary = boundary_ref[...].astype(jnp.float32)
    for s in range(subs):
        for copy in copies[s]:
            copy.wait()
        inverse = inverse_buf[s]
        load = jnp.broadcast_to(interior[s : s + 1], (16, inner_size)).astype(jnp.bfloat16)
        solved = lax.dot_general(
            load, inverse, (((1,), (1,)), ((), ())), preferred_element_type=jnp.float32
        ).astype(jnp.bfloat16)
        carried = jnp.dot(solved, coupling_buf[s], preferred_element_type=jnp.float32)
        condensed = boundary[s : s + 1] - carried[0:1]
        condensed = condensed.astype(jnp.bfloat16).astype(jnp.float32)
        for pair in range(width // (2 * PR)):
            columns = coupling_buf[s, :, pair * 2 * PR : (pair + 1) * 2 * PR]
            inner = jnp.dot(inverse, columns, preferred_element_type=jnp.float32)
            inner = inner.astype(jnp.bfloat16)
            product = lax.dot_general(
                columns, inner, (((0,), (0,)), ((), ())), preferred_element_type=jnp.float32
            )
            for half in range(2):
                k = pair * 2 + half
                item = s * NPS + k
                block = product[half * PR : (half + 1) * PR, half * PR : (half + 1) * PR]
                diagonal = jnp.where(same, stiffness[s : s + 1, k * PR : (k + 1) * PR], 0.0)
                panel = (diagonal - block).astype(jnp.bfloat16)
                panel = jnp.dot(order, panel, preferred_element_type=jnp.float32)
                panel = panel.astype(jnp.bfloat16)
                q = ply_ref[item, 0]
                slot = slot_ref[item]
                rank = count[q]
                count[q] = rank + 1
                for y in range(N_Y):
                    out_ref[y * plies + q, pl.ds(pl.multiple_of(rank * SHARE, SHARE), SHARE), :] = (
                        panel[y * SHARE : (y + 1) * SHARE]
                    )
                extra[q, pl.ds(rank, 1), :] = condensed[:, k * PR : (k + 1) * PR]
                codes = extra[q, CODE_ROW : CODE_ROW + 1, :]
                codes = jnp.where(row_item == rank, (row_code + slot).astype(jnp.float32), codes)
                codes = jnp.where(
                    lane == CAP * SHARE + rank, (LOADS + slot).astype(jnp.float32), codes
                )
                extra[q, CODE_ROW : CODE_ROW + 1, :] = codes
    is_code = iota((8, PR), 0) == CODE_ROW
    for q in range(plies):
        rows = extra[q]
        for y in range(N_Y):
            turned = rows if y == 0 else pltpu.roll(rows, PR - BITS * y, 1)
            out_ref[y * plies + q, CAP * SHARE : CHUNK, :] = jnp.where(
                is_code, rows, turned
            ).astype(jnp.bfloat16)


def combine_kernel(got_ref, out_ref):
    plies = got_ref.shape[0] // N_Y
    sum_rows = iota((LOADS + 8, CHUNK), 0).astype(jnp.float32)
    sums = []
    for y in range(N_Y):
        total = jnp.zeros((LOADS + 8, PR), jnp.float32)
        for q in range(plies):
            message = got_ref[y * plies + q]
            tail = message[CAP * SHARE : CHUNK].astype(jnp.float32)
            codes = tail[CODE_ROW : CODE_ROW + 1, 0:CHUNK]
            choose = (sum_rows == codes).astype(jnp.bfloat16)
            total = total + jnp.dot(choose, message, preferred_element_type=jnp.float32)
        sums.append(total)
    loads = jnp.concatenate([t[LOADS : LOADS + P_OWN] for t in sums], axis=0)
    loads = jnp.concatenate([loads, jnp.zeros((PR - N_Y * P_OWN, PR), jnp.float32)], axis=0)
    loads = loads.T
    step = BITS * P_OWN
    for z in range(N_Z):
        rows = [t[z * step : (z + 1) * step] for t in sums] + [loads[z * step : (z + 1) * step]]
        out_ref[z] = jnp.concatenate(rows, axis=0).astype(jnp.bfloat16)


def place_kernel(target_ref, got_ref, blocks_ref, loads_ref):
    patches = target_ref.shape[1]
    target = target_ref[...]
    rows = N_Y * P_OWN * BITS
    slots = P_OWN - 1
    blocks = got_ref[:, 0:rows, :].reshape(N_Z * rows, PR)
    loads = got_ref[:, rows:BACK, :].astype(jnp.float32).reshape(N_Z * 8, PR)
    loads = loads.astype(jnp.bfloat16)
    for bit in range(BITS):
        wanted = (target - (target & slots)) * BITS + bit * P_OWN + (target & slots)
        choose = (iota((N_Z * rows, patches), 0) == wanted).astype(jnp.bfloat16)
        blocks_ref[0, bit] = lax.dot_general(
            choose, blocks, (((0,), (0,)), ((), ())), preferred_element_type=jnp.float32
        )
        wanted = (target // (N_Y * P_OWN)) * 8 + bit
        choose = (iota((N_Z * 8, patches), 0) == wanted).astype(jnp.bfloat16)
        picked = lax.dot_general(
            loads, choose, (((0,), (0,)), ((), ())), preferred_element_type=jnp.float32
        )[0 : N_Y * P_OWN]
        mine = iota(picked.shape, 0) == target % (N_Y * P_OWN)
        loads_ref[0, bit : bit + 1, :] = jnp.sum(
            jnp.where(mine, picked, 0.0), axis=0, keepdims=True
        )


def vmem():
    return pl.BlockSpec(memory_space=pltpu.VMEM)


def smem():
    return pl.BlockSpec(memory_space=pltpu.SMEM)


def hbm():
    return pl.BlockSpec(memory_space=pl.ANY)


def on_device(
    interior_inverse,
    coupling,
    boundary_stiffness,
    interior_load,
    boundary_load,
    touch_ply,
    touch_slot,
    source_position,
):
    wide_count = lax.axis_size("wide")
    ply_count = lax.axis_size("ply")
    subs, inner_size, width = coupling.shape
    patches = source_position.shape[1]
    params = pltpu.CompilerParams(vmem_limit_bytes=VMEM_LIMIT)
    send = pl.pallas_call(
        condense_kernel,
        out_shape=jax.ShapeDtypeStruct((N_Y * ply_count, CHUNK, PR), jnp.bfloat16),
        in_specs=[smem(), smem(), hbm(), hbm(), vmem(), vmem(), vmem()],
        out_specs=vmem(),
        scratch_shapes=[
            pltpu.VMEM((subs, inner_size, inner_size), jnp.bfloat16),
            pltpu.VMEM((subs, inner_size, width), jnp.bfloat16),
            pltpu.VMEM((ply_count, 8, PR), jnp.float32),
            pltpu.SMEM((ply_count,), jnp.int32),
            pltpu.SemaphoreType.DMA((2, subs)),
        ],
        compiler_params=params,
        name="condense",
    )(
        touch_ply,
        touch_slot,
        interior_inverse,
        coupling,
        boundary_stiffness,
        interior_load,
        boundary_load,
    )
    plane = N_Y * ply_count
    got = lax.all_to_all(
        send,
        ("wide", "ply"),
        split_axis=0,
        concat_axis=0,
        tiled=True,
        axis_index_groups=[[z * plane + i for i in range(plane)] for z in range(N_Z)],
    )
    back = pl.pallas_call(
        combine_kernel,
        out_shape=jax.ShapeDtypeStruct((N_Z, BACK, PR), jnp.bfloat16),
        in_specs=[vmem()],
        out_specs=vmem(),
        compiler_params=params,
        name="combine",
    )(got)
    got = lax.all_to_all(
        back,
        "wide",
        split_axis=0,
        concat_axis=0,
        tiled=True,
        axis_index_groups=[[z * N_Y + y for z in range(N_Z)] for y in range(N_Y)],
    )
    return pl.pallas_call(
        place_kernel,
        out_shape=(
            jax.ShapeDtypeStruct((1, BITS, patches, PR), jnp.float32),
            jax.ShapeDtypeStruct((1, BITS, patches), jnp.float32),
        ),
        in_specs=[vmem(), vmem()],
        out_specs=(vmem(), vmem()),
        compiler_params=params,
        name="place",
    )(source_position, got)


def solution(mesh):
    return jax.shard_map(
        on_device,
        mesh=mesh,
        in_specs=(
            P(("wide", "ply"), None, None),
            P(("wide", "ply"), None, None),
            P(("wide", "ply"), None),
            P(("wide", "ply"), None),
            P(("wide", "ply"), None),
            P(("wide", "ply"), None),
            P(("wide", "ply")),
            P("ply", None),
        ),
        out_specs=(P("ply", "wide", None, None), P("ply", "wide", None)),
        check_vma=False,
    )
```

```python
import jax
import jax.numpy as jnp
from jax import lax
from jax.experimental import pallas as pl
from jax.experimental.pallas import tpu as pltpu
from jax.sharding import PartitionSpec as P

PR = 128
NPS = 4
P_OWN = 4
CAP = 3
N_Z = 16
N_Y = 4
BITS = 2
SHARE = N_Z * BITS
CHUNK = CAP * SHARE + 8
CODE_ROW = CAP
LOADS = SHARE * P_OWN
BACK = N_Y * P_OWN * BITS + 8
VMEM_LIMIT = 40 * 1024 * 1024


def iota(shape, axis):
    return lax.broadcasted_iota(jnp.int32, shape, axis)


def condense_kernel(
    ply_hbm,
    slot_hbm,
    inverse_hbm,
    coupling_hbm,
    stiffness_hbm,
    interior_hbm,
    boundary_hbm,
    out_ref,
    ply_ref,
    slot_ref,
    inverse_buf,
    coupling_buf,
    stiffness_ref,
    interior_ref,
    boundary_ref,
    rows_ref,
    extra,
    count,
    sems,
    small_sems,
):
    subs, inner_size, width = coupling_buf.shape
    plies = extra.shape[0]
    small = [
        pltpu.make_async_copy(source, target, small_sems.at[n])
        for n, (source, target) in enumerate(
            (
                (ply_hbm, ply_ref),
                (slot_hbm, slot_ref),
                (stiffness_hbm, stiffness_ref),
                (interior_hbm, interior_ref),
                (boundary_hbm, boundary_ref),
            )
        )
    ]
    for copy in small:
        copy.start()

    def sub_copies(s):
        return (
            pltpu.make_async_copy(inverse_hbm.at[s], inverse_buf.at[s], sems.at[0, s]),
            pltpu.make_async_copy(coupling_hbm.at[s], coupling_buf.at[s], sems.at[1, s]),
        )

    for s in range(subs):
        for copy in sub_copies(s):
            copy.start()
    out_ref[...] = jnp.zeros_like(out_ref)
    extra[...] = jnp.where(iota(extra.shape, 1) == CODE_ROW, -1.0, 0.0)
    for q in range(plies):
        count[q] = 0
    lane = iota((1, PR), 1)
    row_code = (lane % N_Z) * (BITS * P_OWN) + ((lane // N_Z) % BITS) * P_OWN
    row_item = lane // SHARE
    row = iota((PR, PR), 0)
    source = (row % N_Z) * (N_Y * BITS) + (row // SHARE) * BITS + (row // N_Z) % BITS
    ordered = source == iota((PR, PR), 1)
    wide_row = iota((2 * PR, 2 * PR), 0)
    wide_source = (
        (wide_row % N_Z) * (N_Y * BITS)
        + (wide_row % PR // SHARE) * BITS
        + (wide_row // N_Z) % BITS
        + wide_row // PR * PR
    )
    order = (wide_source == iota((2 * PR, 2 * PR), 1)).astype(jnp.bfloat16)
    for copy in small:
        copy.wait()
    rows_ref[0:subs, 0:width] = stiffness_ref[...].astype(jnp.float32)
    rows_ref[8 : 8 + subs, 0:inner_size] = interior_ref[...].astype(jnp.float32)
    rows_ref[16 : 16 + subs, 0:width] = boundary_ref[...].astype(jnp.float32)

    def subregion(s, carry):
        for copy in sub_copies(s):
            copy.wait()
        stiffness = rows_ref[pl.ds(s, 1), 0:width]
        interior = rows_ref[pl.ds(8 + s, 1), 0:inner_size]
        boundary = rows_ref[pl.ds(16 + s, 1), 0:width]
        load = jnp.broadcast_to(interior, (16, inner_size)).astype(jnp.bfloat16)
        solved = lax.dot_general(
            load, inverse_buf[s], (((1,), (1,)), ((), ())), preferred_element_type=jnp.float32
        ).astype(jnp.bfloat16)
        left = jnp.concatenate([inverse_buf[s], solved], axis=0)
        for pair in range(width // (2 * PR)):
            columns = coupling_buf[s, :, pair * 2 * PR : (pair + 1) * 2 * PR]
            turned = lax.dot_general(
                order, columns, (((1,), (1,)), ((), ())), preferred_element_type=jnp.float32
            ).astype(jnp.bfloat16)
            both = jnp.dot(left, columns, preferred_element_type=jnp.float32)
            inner = both[0:inner_size].astype(jnp.bfloat16)
            condensed = (
                boundary[:, pair * 2 * PR : (pair + 1) * 2 * PR]
                - both[inner_size : inner_size + 1]
            )
            condensed = condensed.astype(jnp.bfloat16).astype(jnp.float32)
            product = jnp.dot(turned, inner, preferred_element_type=jnp.float32)
            for half in range(2):
                k = pair * 2 + half
                item = s * NPS + k
                block = product[half * PR : (half + 1) * PR, half * PR : (half + 1) * PR]
                diagonal = jnp.where(ordered, stiffness[:, k * PR : (k + 1) * PR], 0.0)
                panel = (diagonal - block).astype(jnp.bfloat16)
                q = ply_ref[item]
                slot = slot_ref[item]
                rank = count[q]
                count[q] = rank + 1
                for y in range(N_Y):
                    out_ref[y * plies + q, pl.ds(pl.multiple_of(rank * SHARE, SHARE), SHARE), :] = (
                        panel[y * SHARE : (y + 1) * SHARE]
                    )
                extra[q, pl.ds(rank, 1), :] = condensed[:, half * PR : (half + 1) * PR]
                codes = extra[q, CODE_ROW : CODE_ROW + 1, :]
                codes = jnp.where(row_item == rank, (row_code + slot).astype(jnp.float32), codes)
                codes = jnp.where(
                    lane == CAP * SHARE + rank, (LOADS + slot).astype(jnp.float32), codes
                )
                extra[q, CODE_ROW : CODE_ROW + 1, :] = codes
        return carry

    lax.fori_loop(0, subs, subregion, 0)
    is_code = iota((8, PR), 0) == CODE_ROW
    for q in range(plies):
        rows = extra[q]
        for y in range(N_Y):
            turned = rows if y == 0 else pltpu.roll(rows, PR - BITS * y, 1)
            out_ref[y * plies + q, CAP * SHARE : CHUNK, :] = jnp.where(
                is_code, rows, turned
            ).astype(jnp.bfloat16)


def combine_kernel(got_ref, out_ref):
    plies = got_ref.shape[0] // N_Y
    sum_rows = iota((LOADS + 8, CHUNK), 0).astype(jnp.float32)
    sums = []
    for y in range(N_Y):
        total = jnp.zeros((LOADS + 8, PR), jnp.float32)
        for q in range(plies):
            message = got_ref[y * plies + q]
            tail = message[CAP * SHARE : CHUNK].astype(jnp.float32)
            codes = tail[CODE_ROW : CODE_ROW + 1, 0:CHUNK]
            choose = (sum_rows == codes).astype(jnp.bfloat16)
            total = total + jnp.dot(choose, message, preferred_element_type=jnp.float32)
        sums.append(total)
    loads = jnp.concatenate([t[LOADS : LOADS + P_OWN] for t in sums], axis=0)
    loads = jnp.concatenate([loads, jnp.zeros((PR - N_Y * P_OWN, PR), jnp.float32)], axis=0)
    loads = loads.T
    step = BITS * P_OWN
    for z in range(N_Z):
        rows = [t[z * step : (z + 1) * step] for t in sums] + [loads[z * step : (z + 1) * step]]
        out_ref[z] = jnp.concatenate(rows, axis=0).astype(jnp.bfloat16)


def place_kernel(target_ref, got_ref, blocks_ref, loads_ref):
    patches = target_ref.shape[1]
    target = target_ref[...]
    rows = N_Y * P_OWN * BITS
    slots = P_OWN - 1
    blocks = got_ref[:, 0:rows, :].reshape(N_Z * rows, PR)
    loads = got_ref[:, rows:BACK, :].astype(jnp.float32).reshape(N_Z * 8, PR)
    loads = loads.astype(jnp.bfloat16)
    for bit in range(BITS):
        wanted = (target - (target & slots)) * BITS + bit * P_OWN + (target & slots)
        choose = (iota((N_Z * rows, patches), 0) == wanted).astype(jnp.bfloat16)
        blocks_ref[0, bit] = lax.dot_general(
            choose, blocks, (((0,), (0,)), ((), ())), preferred_element_type=jnp.float32
        )
        wanted = (target // (N_Y * P_OWN)) * 8 + bit
        choose = (iota((N_Z * 8, patches), 0) == wanted).astype(jnp.bfloat16)
        picked = lax.dot_general(
            loads, choose, (((0,), (0,)), ((), ())), preferred_element_type=jnp.float32
        )[0 : N_Y * P_OWN]
        mine = iota(picked.shape, 0) == target % (N_Y * P_OWN)
        loads_ref[0, bit : bit + 1, :] = jnp.sum(
            jnp.where(mine, picked, 0.0), axis=0, keepdims=True
        )


def vmem():
    return pl.BlockSpec(memory_space=pltpu.VMEM)


def condense(*arguments):
    touch_slot, interior_inverse, coupling = arguments[1:4]
    subs, inner_size, width = coupling.shape
    plies = lax.axis_size("ply")
    return pl.pallas_call(
        condense_kernel,
        out_shape=jax.ShapeDtypeStruct((N_Y * plies, CHUNK, PR), jnp.bfloat16),
        in_specs=[pl.BlockSpec(memory_space=pltpu.HBM)] * len(arguments),
        out_specs=vmem(),
        scratch_shapes=[
            pltpu.SMEM(touch_slot.shape, jnp.int32),
            pltpu.SMEM(touch_slot.shape, jnp.int32),
            pltpu.VMEM(interior_inverse.shape, jnp.bfloat16),
            pltpu.VMEM(coupling.shape, jnp.bfloat16),
            pltpu.VMEM((subs, width), jnp.bfloat16),
            pltpu.VMEM((subs, inner_size), jnp.bfloat16),
            pltpu.VMEM((subs, width), jnp.bfloat16),
            pltpu.VMEM((24, inner_size), jnp.float32),
            pltpu.VMEM((plies, 8, PR), jnp.float32),
            pltpu.SMEM((plies,), jnp.int32),
            pltpu.SemaphoreType.DMA((2, subs)),
            pltpu.SemaphoreType.DMA((5,)),
        ],
        compiler_params=pltpu.CompilerParams(vmem_limit_bytes=VMEM_LIMIT),
        name="condense",
    )(*(pltpu.with_memory_space_constraint(argument, pltpu.HBM) for argument in arguments))


def combine(got):
    return pl.pallas_call(
        combine_kernel,
        out_shape=jax.ShapeDtypeStruct((N_Z, BACK, PR), jnp.bfloat16),
        in_specs=[vmem()],
        out_specs=vmem(),
        compiler_params=pltpu.CompilerParams(vmem_limit_bytes=VMEM_LIMIT),
        name="combine",
    )(got)


def place(target, got):
    patches = target.shape[1]
    return pl.pallas_call(
        place_kernel,
        out_shape=(
            jax.ShapeDtypeStruct((1, BITS, patches, PR), jnp.float32),
            jax.ShapeDtypeStruct((1, BITS, patches), jnp.float32),
        ),
        in_specs=[vmem(), vmem()],
        out_specs=(vmem(), vmem()),
        compiler_params=pltpu.CompilerParams(vmem_limit_bytes=VMEM_LIMIT),
        name="place",
    )(target, got)


def on_device(
    interior_inverse,
    coupling,
    boundary_stiffness,
    interior_load,
    boundary_load,
    touch_ply,
    touch_slot,
    source_position,
):
    send = condense(
        touch_ply.reshape(-1),
        touch_slot,
        interior_inverse,
        coupling,
        boundary_stiffness,
        interior_load,
        boundary_load,
    )
    plane = N_Y * lax.axis_size("ply")
    got = lax.all_to_all(
        send,
        ("wide", "ply"),
        split_axis=0,
        concat_axis=0,
        tiled=True,
        axis_index_groups=[[z * plane + i for i in range(plane)] for z in range(N_Z)],
    )
    got = lax.all_to_all(
        combine(got),
        "wide",
        split_axis=0,
        concat_axis=0,
        tiled=True,
        axis_index_groups=[[z * N_Y + y for z in range(N_Z)] for y in range(N_Y)],
    )
    return place(source_position, got)


def solution(mesh):
    return jax.shard_map(
        on_device,
        mesh=mesh,
        in_specs=(
            P(("wide", "ply"), None, None),
            P(("wide", "ply"), None, None),
            P(("wide", "ply"), None),
            P(("wide", "ply"), None),
            P(("wide", "ply"), None),
            P(("wide", "ply"), None),
            P(("wide", "ply")),
            P("ply", None),
        ),
        out_specs=(P("ply", "wide", None, None), P("ply", "wide", None)),
        check_vma=False,
    )
```

```python
import jax
import jax.numpy as jnp
from jax import lax
from jax.experimental import pallas as pl
from jax.experimental.pallas import tpu as pltpu
from jax.sharding import PartitionSpec as P

PR = 128
NPS = 4
P_OWN = 4
CAP = 3
N_Z = 16
N_Y = 4
BITS = 2
SHARE = N_Z * BITS
CHUNK = CAP * SHARE + 8
CODE_ROW = CAP
LOADS = SHARE * P_OWN
BACK = N_Y * P_OWN * BITS + 8
VMEM_LIMIT = 40 * 1024 * 1024


def iota(shape, axis):
    return lax.broadcasted_iota(jnp.int32, shape, axis)


def condense_kernel(
    ply_hbm,
    slot_hbm,
    inverse_hbm,
    coupling_hbm,
    stiffness_hbm,
    interior_hbm,
    boundary_hbm,
    out_ref,
    ply_ref,
    slot_ref,
    inverse_buf,
    coupling_buf,
    stiffness_ref,
    interior_ref,
    boundary_ref,
    rows_ref,
    panels,
    extra,
    count,
    sems,
    small_sems,
):
    subs, inner_size, width = coupling_buf.shape
    plies = extra.shape[0]
    small = [
        pltpu.make_async_copy(source, target, small_sems.at[n])
        for n, (source, target) in enumerate(
            (
                (ply_hbm, ply_ref),
                (slot_hbm, slot_ref),
                (stiffness_hbm, stiffness_ref),
                (interior_hbm, interior_ref),
                (boundary_hbm, boundary_ref),
            )
        )
    ]
    def sub_copies(s):
        return (
            pltpu.make_async_copy(inverse_hbm.at[s], inverse_buf.at[s], sems.at[0, s]),
            pltpu.make_async_copy(coupling_hbm.at[s], coupling_buf.at[s], sems.at[1, s]),
        )

    for copy in (*sub_copies(0), *small, *sub_copies(1)):
        copy.start()
    out_ref[...] = jnp.zeros_like(out_ref)
    extra[...] = jnp.where(iota(extra.shape, 1) == CODE_ROW, -1.0, 0.0)
    for q in range(plies):
        count[q] = 0
    lane = iota((1, PR), 1)
    row_code = (lane % N_Z) * (BITS * P_OWN) + ((lane // N_Z) % BITS) * P_OWN
    row_item = lane // SHARE
    same = iota((PR, PR), 0) == iota((PR, PR), 1)
    for copy in small:
        copy.wait()
    rows_ref[0:subs, 0:width] = stiffness_ref[...].astype(jnp.float32)
    rows_ref[8 : 8 + subs, 0:inner_size] = interior_ref[...].astype(jnp.float32)
    rows_ref[16 : 16 + subs, 0:width] = boundary_ref[...].astype(jnp.float32)

    def subregion(s, carry):
        for copy in sub_copies(s):
            copy.wait()

        @pl.when(s + 2 < subs)
        def _():
            for copy in sub_copies(s + 2):
                copy.start()

        stiffness = rows_ref[pl.ds(s, 1), 0:width]
        interior = rows_ref[pl.ds(8 + s, 1), 0:inner_size]
        boundary = rows_ref[pl.ds(16 + s, 1), 0:width]
        inverse = inverse_buf[s]
        coupling = coupling_buf[s]
        turned = coupling.T
        solved = jnp.sum(inverse.astype(jnp.float32) * interior, axis=1, keepdims=True)
        solved = solved.astype(jnp.bfloat16).astype(jnp.float32)
        inner = jnp.dot(inverse, coupling, preferred_element_type=jnp.float32)
        inner = inner.astype(jnp.bfloat16)
        carried = jnp.sum(coupling.astype(jnp.float32) * solved, axis=0, keepdims=True)
        condensed = (boundary - carried).astype(jnp.bfloat16).astype(jnp.float32)
        for k in range(NPS):
            columns = slice(k * PR, (k + 1) * PR)
            product = jnp.dot(
                turned[columns], inner[:, columns], preferred_element_type=jnp.float32
            )
            panels[columns, :] = jnp.where(same, stiffness[:, columns], 0.0) - product
        for k in range(NPS):
            item = s * NPS + k
            q = ply_ref[item]
            slot = slot_ref[item]
            rank = count[q]
            count[q] = rank + 1
            for y in range(N_Y):
                part = [
                    panels[pl.ds(k * PR + y * BITS + bit, N_Z, stride=N_Y * BITS), :]
                    for bit in range(BITS)
                ]
                out_ref[y * plies + q, pl.ds(pl.multiple_of(rank * SHARE, SHARE), SHARE), :] = (
                    jnp.concatenate(part, axis=0).astype(jnp.bfloat16)
                )
            extra[q, pl.ds(rank, 1), :] = condensed[:, k * PR : (k + 1) * PR]
            codes = extra[q, CODE_ROW : CODE_ROW + 1, :]
            codes = jnp.where(row_item == rank, (row_code + slot).astype(jnp.float32), codes)
            codes = jnp.where(
                lane == CAP * SHARE + rank, (LOADS + slot).astype(jnp.float32), codes
            )
            extra[q, CODE_ROW : CODE_ROW + 1, :] = codes
        return carry

    lax.fori_loop(0, subs, subregion, 0)
    is_code = iota((8, PR), 0) == CODE_ROW
    for q in range(plies):
        rows = extra[q]
        for y in range(N_Y):
            turned = rows if y == 0 else pltpu.roll(rows, PR - BITS * y, 1)
            out_ref[y * plies + q, CAP * SHARE : CHUNK, :] = jnp.where(
                is_code, rows, turned
            ).astype(jnp.bfloat16)


def combine_kernel(got_ref, out_ref):
    plies = got_ref.shape[0] // N_Y
    sum_rows = iota((LOADS + 8, CHUNK), 0).astype(jnp.float32)
    sums = []
    for y in range(N_Y):
        total = jnp.zeros((LOADS + 8, PR), jnp.float32)
        for q in range(plies):
            message = got_ref[y * plies + q]
            tail = message[CAP * SHARE : CHUNK].astype(jnp.float32)
            codes = tail[CODE_ROW : CODE_ROW + 1, 0:CHUNK]
            choose = (sum_rows == codes).astype(jnp.bfloat16)
            total = total + jnp.dot(choose, message, preferred_element_type=jnp.float32)
        sums.append(total)
    loads = jnp.concatenate([t[LOADS : LOADS + P_OWN] for t in sums], axis=0)
    loads = jnp.concatenate([loads, jnp.zeros((PR - N_Y * P_OWN, PR), jnp.float32)], axis=0)
    loads = loads.T
    step = BITS * P_OWN
    for z in range(N_Z):
        rows = [t[z * step : (z + 1) * step] for t in sums] + [loads[z * step : (z + 1) * step]]
        out_ref[z] = jnp.concatenate(rows, axis=0).astype(jnp.bfloat16)


def place_kernel(target_ref, got_ref, blocks_ref, loads_ref):
    patches = target_ref.shape[1]
    target = target_ref[...]
    rows = N_Y * P_OWN * BITS
    slots = P_OWN - 1
    blocks = got_ref[:, 0:rows, :].reshape(N_Z * rows, PR)
    loads = got_ref[:, rows:BACK, :].astype(jnp.float32).reshape(N_Z * 8, PR)
    loads = loads.astype(jnp.bfloat16)
    for bit in range(BITS):
        wanted = (target - (target & slots)) * BITS + bit * P_OWN + (target & slots)
        choose = (iota((N_Z * rows, patches), 0) == wanted).astype(jnp.bfloat16)
        blocks_ref[0, bit] = lax.dot_general(
            choose, blocks, (((0,), (0,)), ((), ())), preferred_element_type=jnp.float32
        )
        wanted = (target // (N_Y * P_OWN)) * 8 + bit
        choose = (iota((N_Z * 8, patches), 0) == wanted).astype(jnp.bfloat16)
        picked = lax.dot_general(
            loads, choose, (((0,), (0,)), ((), ())), preferred_element_type=jnp.float32
        )[0 : N_Y * P_OWN]
        mine = iota(picked.shape, 0) == target % (N_Y * P_OWN)
        loads_ref[0, bit : bit + 1, :] = jnp.sum(
            jnp.where(mine, picked, 0.0), axis=0, keepdims=True
        )


def vmem():
    return pl.BlockSpec(memory_space=pltpu.VMEM)


def condense(*arguments):
    touch_slot, interior_inverse, coupling = arguments[1:4]
    subs, inner_size, width = coupling.shape
    plies = lax.axis_size("ply")
    return pl.pallas_call(
        condense_kernel,
        out_shape=jax.ShapeDtypeStruct((N_Y * plies, CHUNK, PR), jnp.bfloat16),
        in_specs=[pl.BlockSpec(memory_space=pltpu.HBM)] * len(arguments),
        out_specs=vmem(),
        scratch_shapes=[
            pltpu.SMEM(touch_slot.shape, jnp.int32),
            pltpu.SMEM(touch_slot.shape, jnp.int32),
            pltpu.VMEM(interior_inverse.shape, jnp.bfloat16),
            pltpu.VMEM(coupling.shape, jnp.bfloat16),
            pltpu.VMEM((subs, width), jnp.bfloat16),
            pltpu.VMEM((subs, inner_size), jnp.bfloat16),
            pltpu.VMEM((subs, width), jnp.bfloat16),
            pltpu.VMEM((24, inner_size), jnp.float32),
            pltpu.VMEM((width, PR), jnp.float32),
            pltpu.VMEM((plies, 8, PR), jnp.float32),
            pltpu.SMEM((plies,), jnp.int32),
            pltpu.SemaphoreType.DMA((2, subs)),
            pltpu.SemaphoreType.DMA((5,)),
        ],
        compiler_params=pltpu.CompilerParams(vmem_limit_bytes=VMEM_LIMIT),
        name="condense",
    )(*(pltpu.with_memory_space_constraint(argument, pltpu.HBM) for argument in arguments))


def combine(got):
    return pl.pallas_call(
        combine_kernel,
        out_shape=jax.ShapeDtypeStruct((N_Z, BACK, PR), jnp.bfloat16),
        in_specs=[vmem()],
        out_specs=vmem(),
        compiler_params=pltpu.CompilerParams(vmem_limit_bytes=VMEM_LIMIT),
        name="combine",
    )(got)


def place(target, got):
    patches = target.shape[1]
    return pl.pallas_call(
        place_kernel,
        out_shape=(
            jax.ShapeDtypeStruct((1, BITS, patches, PR), jnp.float32),
            jax.ShapeDtypeStruct((1, BITS, patches), jnp.float32),
        ),
        in_specs=[vmem(), vmem()],
        out_specs=(vmem(), vmem()),
        compiler_params=pltpu.CompilerParams(vmem_limit_bytes=VMEM_LIMIT),
        name="place",
    )(target, got)


def on_device(
    interior_inverse,
    coupling,
    boundary_stiffness,
    interior_load,
    boundary_load,
    touch_ply,
    touch_slot,
    source_position,
):
    send = condense(
        touch_ply.reshape(-1),
        touch_slot,
        interior_inverse,
        coupling,
        boundary_stiffness,
        interior_load,
        boundary_load,
    )
    plane = N_Y * lax.axis_size("ply")
    got = lax.all_to_all(
        send,
        ("wide", "ply"),
        split_axis=0,
        concat_axis=0,
        tiled=True,
        axis_index_groups=[[z * plane + i for i in range(plane)] for z in range(N_Z)],
    )
    got = lax.all_to_all(
        combine(got),
        "wide",
        split_axis=0,
        concat_axis=0,
        tiled=True,
        axis_index_groups=[[z * N_Y + y for z in range(N_Z)] for y in range(N_Y)],
    )
    return place(source_position, got)


def solution(mesh):
    return jax.shard_map(
        on_device,
        mesh=mesh,
        in_specs=(
            P(("wide", "ply"), None, None),
            P(("wide", "ply"), None, None),
            P(("wide", "ply"), None),
            P(("wide", "ply"), None),
            P(("wide", "ply"), None),
            P(("wide", "ply"), None),
            P(("wide", "ply")),
            P("ply", None),
        ),
        out_specs=(P("ply", "wide", None, None), P("ply", "wide", None)),
        check_vma=False,
    )
```

```python
import jax
import jax.numpy as jnp
from jax import lax
from jax.experimental import pallas as pl
from jax.experimental.pallas import tpu as pltpu
from jax.sharding import PartitionSpec as P

PR = 128
NPS = 4
P_OWN = 4
CAP = 3
N_Z = 16
N_Y = 4
BITS = 2
SHARE = N_Z * BITS
CHUNK = CAP * SHARE + 8
CODE_ROW = CAP
LOADS = SHARE * P_OWN
BACK = N_Y * P_OWN * BITS + 8
FIRST_Z = 10
LAST = 11
VMEM_LIMIT = 40 * 1024 * 1024


def iota(shape, axis):
    return lax.broadcasted_iota(jnp.int32, shape, axis)


def condense_kernel(
    ply_hbm,
    slot_hbm,
    inverse_hbm,
    coupling_hbm,
    stiffness_hbm,
    interior_hbm,
    boundary_hbm,
    out_ref,
    ply_ref,
    slot_ref,
    inverse_buf,
    coupling_buf,
    stiffness_ref,
    interior_ref,
    boundary_ref,
    rows_ref,
    panels,
    extra,
    count,
    sems,
    small_sems,
):
    subs, inner_size, width = coupling_buf.shape
    plies = extra.shape[0]
    small = [
        pltpu.make_async_copy(source, target, small_sems.at[n])
        for n, (source, target) in enumerate(
            (
                (ply_hbm, ply_ref),
                (slot_hbm, slot_ref),
                (stiffness_hbm, stiffness_ref),
                (interior_hbm, interior_ref),
                (boundary_hbm, boundary_ref),
            )
        )
    ]
    def sub_copies(s):
        return (
            pltpu.make_async_copy(inverse_hbm.at[s], inverse_buf.at[s], sems.at[0, s]),
            pltpu.make_async_copy(coupling_hbm.at[s], coupling_buf.at[s], sems.at[1, s]),
        )

    for copy in (*sub_copies(0), *small, *sub_copies(1)):
        copy.start()
    out_ref[...] = jnp.zeros_like(out_ref)
    extra[...] = jnp.where(iota(extra.shape, 1) == CODE_ROW, -1.0, 0.0)
    for q in range(plies):
        count[q] = 0
    lane = iota((1, PR), 1)
    row_code = (lane % N_Z) * (BITS * P_OWN) + ((lane // N_Z) % BITS) * P_OWN
    row_item = lane // SHARE
    same = iota((PR, PR), 0) == iota((PR, PR), 1)
    for copy in small:
        copy.wait()
    rows_ref[0:subs, 0:width] = stiffness_ref[...].astype(jnp.float32)
    rows_ref[8 : 8 + subs, 0:inner_size] = interior_ref[...].astype(jnp.float32)
    rows_ref[16 : 16 + subs, 0:width] = boundary_ref[...].astype(jnp.float32)

    def subregion(s, carry):
        for copy in sub_copies(s):
            copy.wait()

        @pl.when(s + 2 < subs)
        def _():
            for copy in sub_copies(s + 2):
                copy.start()

        stiffness = rows_ref[pl.ds(s, 1), 0:width]
        interior = rows_ref[pl.ds(8 + s, 1), 0:inner_size]
        boundary = rows_ref[pl.ds(16 + s, 1), 0:width]
        inverse = inverse_buf[s]
        coupling = coupling_buf[s]
        turned = coupling.T
        solved = jnp.sum(inverse.astype(jnp.float32) * interior, axis=1, keepdims=True)
        solved = solved.astype(jnp.bfloat16).astype(jnp.float32)
        inner = jnp.dot(inverse, coupling, preferred_element_type=jnp.float32)
        inner = inner.astype(jnp.bfloat16)
        carried = jnp.sum(coupling.astype(jnp.float32) * solved, axis=0, keepdims=True)
        condensed = (boundary - carried).astype(jnp.bfloat16).astype(jnp.float32)
        for k in range(NPS):
            columns = slice(k * PR, (k + 1) * PR)
            product = jnp.dot(
                turned[columns], inner[:, columns], preferred_element_type=jnp.float32
            )
            panels[columns, :] = jnp.where(same, stiffness[:, columns], 0.0) - product
        for k in range(NPS):
            item = s * NPS + k
            q = ply_ref[item]
            slot = slot_ref[item]
            rank = count[q]
            count[q] = rank + 1
            for y in range(N_Y):
                part = [
                    panels[pl.ds(k * PR + y * BITS + bit, N_Z, stride=N_Y * BITS), :]
                    for bit in range(BITS)
                ]
                place = lax.rem(y * plies + q + LAST, N_Y * plies)
                out_ref[place, pl.ds(pl.multiple_of(rank * SHARE, SHARE), SHARE), :] = (
                    jnp.concatenate(part, axis=0).astype(jnp.bfloat16)
                )
            extra[q, pl.ds(rank, 1), :] = condensed[:, k * PR : (k + 1) * PR]
            codes = extra[q, CODE_ROW : CODE_ROW + 1, :]
            codes = jnp.where(row_item == rank, (row_code + slot).astype(jnp.float32), codes)
            codes = jnp.where(
                lane == CAP * SHARE + rank, (LOADS + slot).astype(jnp.float32), codes
            )
            extra[q, CODE_ROW : CODE_ROW + 1, :] = codes
        return carry

    lax.fori_loop(0, subs, subregion, 0)
    is_code = iota((8, PR), 0) == CODE_ROW
    for q in range(plies):
        rows = extra[q]
        for y in range(N_Y):
            turned = rows if y == 0 else pltpu.roll(rows, PR - BITS * y, 1)
            place = (y * plies + q + LAST) % (N_Y * plies)
            out_ref[place, CAP * SHARE : CHUNK, :] = jnp.where(
                is_code, rows, turned
            ).astype(jnp.bfloat16)


def combine_kernel(got_ref, out_ref):
    plies = got_ref.shape[0] // N_Y
    sum_rows = iota((LOADS + 8, CHUNK), 0).astype(jnp.float32)
    sums = []
    for y in range(N_Y):
        total = jnp.zeros((LOADS + 8, PR), jnp.float32)
        for q in range(plies):
            message = got_ref[(y * plies + q + LAST) % (N_Y * plies)]
            tail = message[CAP * SHARE : CHUNK].astype(jnp.float32)
            codes = tail[CODE_ROW : CODE_ROW + 1, 0:CHUNK]
            choose = (sum_rows == codes).astype(jnp.bfloat16)
            total = total + jnp.dot(choose, message, preferred_element_type=jnp.float32)
        sums.append(total)
    loads = jnp.concatenate([t[LOADS : LOADS + P_OWN] for t in sums], axis=0)
    loads = jnp.concatenate([loads, jnp.zeros((PR - N_Y * P_OWN, PR), jnp.float32)], axis=0)
    loads = loads.T
    step = BITS * P_OWN
    for z in range(N_Z):
        rows = [t[z * step : (z + 1) * step] for t in sums] + [loads[z * step : (z + 1) * step]]
        out_ref[(z - FIRST_Z) % N_Z] = jnp.concatenate(rows, axis=0).astype(jnp.bfloat16)


def place_kernel(target_ref, got_ref, blocks_ref, loads_ref):
    patches = target_ref.shape[1]
    z_owners = N_Y * P_OWN
    target = lax.rem(target_ref[...] + (N_Z - FIRST_Z) * z_owners, N_Z * z_owners)
    rows = N_Y * P_OWN * BITS
    slots = P_OWN - 1
    blocks = got_ref[:, 0:rows, :].reshape(N_Z * rows, PR)
    loads = got_ref[:, rows:BACK, :].astype(jnp.float32).reshape(N_Z * 8, PR)
    loads = loads.astype(jnp.bfloat16)
    for bit in range(BITS):
        wanted = (target - (target & slots)) * BITS + bit * P_OWN + (target & slots)
        choose = (iota((N_Z * rows, patches), 0) == wanted).astype(jnp.bfloat16)
        blocks_ref[0, bit] = lax.dot_general(
            choose, blocks, (((0,), (0,)), ((), ())), preferred_element_type=jnp.float32
        )
        wanted = (target // z_owners) * 8 + bit
        choose = (iota((N_Z * 8, patches), 0) == wanted).astype(jnp.bfloat16)
        picked = lax.dot_general(
            loads, choose, (((0,), (0,)), ((), ())), preferred_element_type=jnp.float32
        )[0:z_owners]
        mine = iota(picked.shape, 0) == target % z_owners
        loads_ref[0, bit : bit + 1, :] = jnp.sum(
            jnp.where(mine, picked, 0.0), axis=0, keepdims=True
        )


def vmem():
    return pl.BlockSpec(memory_space=pltpu.VMEM)


def condense(*arguments):
    touch_slot, interior_inverse, coupling = arguments[1:4]
    subs, inner_size, width = coupling.shape
    plies = lax.axis_size("ply")
    return pl.pallas_call(
        condense_kernel,
        out_shape=jax.ShapeDtypeStruct((N_Y * plies, CHUNK, PR), jnp.bfloat16),
        in_specs=[pl.BlockSpec(memory_space=pltpu.HBM)] * len(arguments),
        out_specs=vmem(),
        scratch_shapes=[
            pltpu.SMEM(touch_slot.shape, jnp.int32),
            pltpu.SMEM(touch_slot.shape, jnp.int32),
            pltpu.VMEM(interior_inverse.shape, jnp.bfloat16),
            pltpu.VMEM(coupling.shape, jnp.bfloat16),
            pltpu.VMEM((subs, width), jnp.bfloat16),
            pltpu.VMEM((subs, inner_size), jnp.bfloat16),
            pltpu.VMEM((subs, width), jnp.bfloat16),
            pltpu.VMEM((24, inner_size), jnp.float32),
            pltpu.VMEM((width, PR), jnp.float32),
            pltpu.VMEM((plies, 8, PR), jnp.float32),
            pltpu.SMEM((plies,), jnp.int32),
            pltpu.SemaphoreType.DMA((2, subs)),
            pltpu.SemaphoreType.DMA((5,)),
        ],
        compiler_params=pltpu.CompilerParams(vmem_limit_bytes=VMEM_LIMIT),
        name="condense",
    )(*(pltpu.with_memory_space_constraint(argument, pltpu.HBM) for argument in arguments))


def combine(got):
    return pl.pallas_call(
        combine_kernel,
        out_shape=jax.ShapeDtypeStruct((N_Z, BACK, PR), jnp.bfloat16),
        in_specs=[vmem()],
        out_specs=vmem(),
        compiler_params=pltpu.CompilerParams(vmem_limit_bytes=VMEM_LIMIT),
        name="combine",
    )(got)


def place(target, got):
    patches = target.shape[1]
    return pl.pallas_call(
        place_kernel,
        out_shape=(
            jax.ShapeDtypeStruct((1, BITS, patches, PR), jnp.float32),
            jax.ShapeDtypeStruct((1, BITS, patches), jnp.float32),
        ),
        in_specs=[vmem(), vmem()],
        out_specs=(vmem(), vmem()),
        compiler_params=pltpu.CompilerParams(vmem_limit_bytes=VMEM_LIMIT),
        name="place",
    )(target, got)


def on_device(
    interior_inverse,
    coupling,
    boundary_stiffness,
    interior_load,
    boundary_load,
    touch_ply,
    touch_slot,
    source_position,
):
    send = condense(
        touch_ply.reshape(-1),
        touch_slot,
        interior_inverse,
        coupling,
        boundary_stiffness,
        interior_load,
        boundary_load,
    )
    plane = N_Y * lax.axis_size("ply")
    got = lax.all_to_all(
        send,
        ("wide", "ply"),
        split_axis=0,
        concat_axis=0,
        tiled=True,
        axis_index_groups=[
            [z * plane + (i - LAST) % plane for i in range(plane)] for z in range(N_Z)
        ],
    )
    got = lax.all_to_all(
        combine(got),
        "wide",
        split_axis=0,
        concat_axis=0,
        tiled=True,
        axis_index_groups=[
            [(i + FIRST_Z) % N_Z * N_Y + y for i in range(N_Z)] for y in range(N_Y)
        ],
    )
    return place(source_position, got)


def solution(mesh):
    return jax.shard_map(
        on_device,
        mesh=mesh,
        in_specs=(
            P(("wide", "ply"), None, None),
            P(("wide", "ply"), None, None),
            P(("wide", "ply"), None),
            P(("wide", "ply"), None),
            P(("wide", "ply"), None),
            P(("wide", "ply"), None),
            P(("wide", "ply")),
            P("ply", None),
        ),
        out_specs=(P("ply", "wide", None, None), P("ply", "wide", None)),
        check_vma=False,
    )
```

```python
import jax
import jax.numpy as jnp
from jax import lax
from jax.experimental import pallas as pl
from jax.experimental.pallas import tpu as pltpu
from jax.sharding import PartitionSpec as P

PR = 128
NPS = 4
P_OWN = 4
CAP = 3
N_Z = 16
N_Y = 4
BITS = 2
SHARE = N_Z * BITS
CHUNK = CAP * SHARE + 8
CODE_ROW = CAP
LOADS = SHARE * P_OWN
QUAD = 4
BACK = N_Y * P_OWN * BITS + QUAD
FIRST_Z = 10
LAST = 11
VMEM_LIMIT = 40 * 1024 * 1024


def iota(shape, axis):
    return lax.broadcasted_iota(jnp.int32, shape, axis)


def condense_kernel(
    ply_hbm,
    slot_hbm,
    inverse_hbm,
    coupling_hbm,
    stiffness_hbm,
    interior_hbm,
    boundary_hbm,
    out_ref,
    ply_ref,
    slot_ref,
    inverse_buf,
    coupling_buf,
    stiffness_ref,
    interior_ref,
    boundary_ref,
    rows_ref,
    panels,
    extra,
    count,
    sems,
    small_sems,
):
    subs, inner_size, width = coupling_buf.shape
    plies = extra.shape[0]
    small = [
        pltpu.make_async_copy(source, target, small_sems.at[n])
        for n, (source, target) in enumerate(
            (
                (ply_hbm, ply_ref),
                (slot_hbm, slot_ref),
                (stiffness_hbm, stiffness_ref),
                (interior_hbm, interior_ref),
                (boundary_hbm, boundary_ref),
            )
        )
    ]
    def sub_copies(s):
        return (
            pltpu.make_async_copy(inverse_hbm.at[s], inverse_buf.at[s], sems.at[0, s]),
            pltpu.make_async_copy(coupling_hbm.at[s], coupling_buf.at[s], sems.at[1, s]),
        )

    for copy in (*sub_copies(0), *small, *sub_copies(1)):
        copy.start()
    out_ref[...] = jnp.zeros_like(out_ref)
    extra[...] = jnp.where(iota(extra.shape, 1) == CODE_ROW, -1.0, 0.0)
    for q in range(plies):
        count[q] = 0
    lane = iota((1, PR), 1)
    row_code = (lane % N_Z) * (BITS * P_OWN) + ((lane // N_Z) % BITS) * P_OWN
    row_item = lane // SHARE
    same = iota((PR, PR), 0) == iota((PR, PR), 1)
    for copy in small:
        copy.wait()
    rows_ref[0:subs, 0:width] = stiffness_ref[...].astype(jnp.float32)
    rows_ref[8 : 8 + subs, 0:inner_size] = interior_ref[...].astype(jnp.float32)
    rows_ref[16 : 16 + subs, 0:width] = boundary_ref[...].astype(jnp.float32)

    def subregion(s, carry):
        for copy in sub_copies(s):
            copy.wait()

        @pl.when(s + 2 < subs)
        def _():
            for copy in sub_copies(s + 2):
                copy.start()

        stiffness = rows_ref[pl.ds(s, 1), 0:width]
        interior = rows_ref[pl.ds(8 + s, 1), 0:inner_size]
        boundary = rows_ref[pl.ds(16 + s, 1), 0:width]
        inverse = inverse_buf[s]
        coupling = coupling_buf[s]
        turned = coupling.T
        solved = jnp.sum(inverse.astype(jnp.float32) * interior, axis=1, keepdims=True)
        solved = solved.astype(jnp.bfloat16).astype(jnp.float32)
        inner = jnp.dot(inverse, coupling, preferred_element_type=jnp.float32)
        inner = inner.astype(jnp.bfloat16)
        carried = jnp.sum(coupling.astype(jnp.float32) * solved, axis=0, keepdims=True)
        condensed = (boundary - carried).astype(jnp.bfloat16).astype(jnp.float32)
        for k in range(NPS):
            columns = slice(k * PR, (k + 1) * PR)
            product = jnp.dot(
                turned[columns], inner[:, columns], preferred_element_type=jnp.float32
            )
            panels[columns, :] = jnp.where(same, stiffness[:, columns], 0.0) - product
        for k in range(NPS):
            item = s * NPS + k
            q = ply_ref[item]
            slot = slot_ref[item]
            rank = count[q]
            count[q] = rank + 1
            for y in range(N_Y):
                part = [
                    panels[pl.ds(k * PR + y * BITS + bit, N_Z, stride=N_Y * BITS), :]
                    for bit in range(BITS)
                ]
                place = lax.rem(y * plies + q + LAST, N_Y * plies)
                out_ref[place, pl.ds(pl.multiple_of(rank * SHARE, SHARE), SHARE), :] = (
                    jnp.concatenate(part, axis=0).astype(jnp.bfloat16)
                )
            extra[q, pl.ds(rank, 1), :] = condensed[:, k * PR : (k + 1) * PR]
            codes = extra[q, CODE_ROW : CODE_ROW + 1, :]
            codes = jnp.where(row_item == rank, (row_code + slot).astype(jnp.float32), codes)
            codes = jnp.where(
                lane == CAP * SHARE + rank, (LOADS + slot).astype(jnp.float32), codes
            )
            extra[q, CODE_ROW : CODE_ROW + 1, :] = codes
        return carry

    lax.fori_loop(0, subs, subregion, 0)
    is_code = iota((8, PR), 0) == CODE_ROW
    for q in range(plies):
        rows = extra[q]
        for y in range(N_Y):
            turned = rows if y == 0 else pltpu.roll(rows, PR - BITS * y, 1)
            place = (y * plies + q + LAST) % (N_Y * plies)
            out_ref[place, CAP * SHARE : CHUNK, :] = jnp.where(
                is_code, rows, turned
            ).astype(jnp.bfloat16)


def combine_kernel(got_ref, out_ref):
    plies = got_ref.shape[0] // N_Y
    sum_rows = iota((LOADS + 8, plies * PR), 0).astype(jnp.float32)
    sums = []
    for y in range(N_Y):
        messages = [got_ref[(y * plies + q + LAST) % (N_Y * plies)] for q in range(plies)]
        codes = jnp.concatenate(
            [
                m[CAP * SHARE : CHUNK].astype(jnp.float32)[CODE_ROW : CODE_ROW + 1]
                for m in messages
            ],
            axis=1,
        )
        choose = (sum_rows == codes).astype(jnp.bfloat16)
        pad = jnp.zeros((PR - CHUNK, PR), jnp.bfloat16)
        rows = jnp.concatenate([v for m in messages for v in (m, pad)], axis=0)
        sums.append(jnp.dot(choose, rows, preferred_element_type=jnp.float32))
    loads = jnp.concatenate([t[LOADS : LOADS + P_OWN] for t in sums], axis=0)
    loads = jnp.concatenate([loads, jnp.zeros((PR - N_Y * P_OWN, PR), jnp.float32)], axis=0)
    loads = loads.T
    step = BITS * P_OWN
    for z in range(N_Z):
        place = (z - FIRST_Z) % N_Z
        rows = [t[z * step : (z + 1) * step] for t in sums] + [loads[z * step : z * step + QUAD]]
        for n, row in enumerate(rows):
            for half in range(row.shape[0] // QUAD):
                out_ref[place, n * (step // QUAD) + half] = row[
                    half * QUAD : (half + 1) * QUAD
                ].astype(jnp.bfloat16)


def place_kernel(target_ref, got_ref, blocks_ref, loads_ref, got_blocks, got_loads):
    patches = target_ref.shape[1]
    z_owners = N_Y * P_OWN
    target = lax.rem(target_ref[...] + (N_Z - FIRST_Z) * z_owners, N_Z * z_owners)
    rows = N_Y * P_OWN * BITS
    got_loads[...] = jnp.zeros_like(got_loads)
    for z in range(N_Z):
        for n in range(rows // QUAD):
            owner = z * z_owners + n // BITS * QUAD
            got_blocks[n % BITS, owner : owner + QUAD, :] = got_ref[z, n].astype(jnp.float32)
        got_loads[z * 8 : z * 8 + QUAD, :] = got_ref[z, rows // QUAD].astype(jnp.float32)
    loads = got_loads[...].astype(jnp.bfloat16)
    choose_owner = jnp.where(iota((patches, patches), 0) == target, 1.0, 0.0).astype(jnp.bfloat16)
    for bit in range(BITS):
        blocks_ref[0, bit] = lax.dot_general(
            choose_owner,
            got_blocks[bit].astype(jnp.bfloat16),
            (((0,), (0,)), ((), ())),
            preferred_element_type=jnp.float32,
        )
        wanted = (target // z_owners) * 8 + bit
        choose = jnp.where(iota((N_Z * 8, patches), 0) == wanted, 1.0, 0.0).astype(jnp.bfloat16)
        picked = lax.dot_general(
            loads, choose, (((0,), (0,)), ((), ())), preferred_element_type=jnp.float32
        )[0:z_owners]
        mine = iota(picked.shape, 0) == target % z_owners
        loads_ref[0, bit : bit + 1, :] = jnp.sum(
            jnp.where(mine, picked, 0.0), axis=0, keepdims=True
        )


def vmem():
    return pl.BlockSpec(memory_space=pltpu.VMEM)


def condense(*arguments):
    touch_slot, interior_inverse, coupling = arguments[1:4]
    subs, inner_size, width = coupling.shape
    plies = lax.axis_size("ply")
    return pl.pallas_call(
        condense_kernel,
        out_shape=jax.ShapeDtypeStruct((N_Y * plies, CHUNK, PR), jnp.bfloat16),
        in_specs=[pl.BlockSpec(memory_space=pltpu.HBM)] * len(arguments),
        out_specs=vmem(),
        scratch_shapes=[
            pltpu.SMEM(touch_slot.shape, jnp.int32),
            pltpu.SMEM(touch_slot.shape, jnp.int32),
            pltpu.VMEM(interior_inverse.shape, jnp.bfloat16),
            pltpu.VMEM(coupling.shape, jnp.bfloat16),
            pltpu.VMEM((subs, width), jnp.bfloat16),
            pltpu.VMEM((subs, inner_size), jnp.bfloat16),
            pltpu.VMEM((subs, width), jnp.bfloat16),
            pltpu.VMEM((24, inner_size), jnp.float32),
            pltpu.VMEM((width, PR), jnp.float32),
            pltpu.VMEM((plies, 8, PR), jnp.float32),
            pltpu.SMEM((plies,), jnp.int32),
            pltpu.SemaphoreType.DMA((2, subs)),
            pltpu.SemaphoreType.DMA((5,)),
        ],
        compiler_params=pltpu.CompilerParams(vmem_limit_bytes=VMEM_LIMIT),
        name="condense",
    )(*(pltpu.with_memory_space_constraint(argument, pltpu.HBM) for argument in arguments))


def combine(got):
    return pl.pallas_call(
        combine_kernel,
        out_shape=jax.ShapeDtypeStruct((N_Z, BACK // QUAD, QUAD, PR), jnp.bfloat16),
        in_specs=[vmem()],
        out_specs=vmem(),
        compiler_params=pltpu.CompilerParams(vmem_limit_bytes=VMEM_LIMIT),
        name="combine",
    )(got)


def place(target, got):
    patches = target.shape[1]
    return pl.pallas_call(
        place_kernel,
        out_shape=(
            jax.ShapeDtypeStruct((1, BITS, patches, PR), jnp.float32),
            jax.ShapeDtypeStruct((1, BITS, patches), jnp.float32),
        ),
        in_specs=[vmem(), vmem()],
        out_specs=(vmem(), vmem()),
        scratch_shapes=[
            pltpu.VMEM((BITS, patches, PR), jnp.float32),
            pltpu.VMEM((N_Z * 8, PR), jnp.float32),
        ],
        compiler_params=pltpu.CompilerParams(vmem_limit_bytes=VMEM_LIMIT),
        name="place",
    )(target, got)


def on_device(
    interior_inverse,
    coupling,
    boundary_stiffness,
    interior_load,
    boundary_load,
    touch_ply,
    touch_slot,
    source_position,
):
    send = condense(
        touch_ply.reshape(-1),
        touch_slot,
        interior_inverse,
        coupling,
        boundary_stiffness,
        interior_load,
        boundary_load,
    )
    plane = N_Y * lax.axis_size("ply")
    got = lax.all_to_all(
        send,
        ("wide", "ply"),
        split_axis=0,
        concat_axis=0,
        tiled=True,
        axis_index_groups=[
            [z * plane + (i - LAST) % plane for i in range(plane)] for z in range(N_Z)
        ],
    )
    got = lax.all_to_all(
        combine(got),
        "wide",
        split_axis=0,
        concat_axis=0,
        tiled=True,
        axis_index_groups=[
            [(i + FIRST_Z) % N_Z * N_Y + y for i in range(N_Z)] for y in range(N_Y)
        ],
    )
    return place(source_position, got)


def solution(mesh):
    return jax.shard_map(
        on_device,
        mesh=mesh,
        in_specs=(
            P(("wide", "ply"), None, None),
            P(("wide", "ply"), None, None),
            P(("wide", "ply"), None),
            P(("wide", "ply"), None),
            P(("wide", "ply"), None),
            P(("wide", "ply"), None),
            P(("wide", "ply")),
            P("ply", None),
        ),
        out_specs=(P("ply", "wide", None, None), P("ply", "wide", None)),
        check_vma=False,
    )
```

```python
import jax
import jax.numpy as jnp
from jax import lax
from jax.experimental import pallas as pl
from jax.experimental.pallas import tpu as pltpu
from jax.sharding import PartitionSpec as P

PR = 128
NPS = 4
P_OWN = 4
N_Z = 16
N_Y = 4
CORES = 2
BITS = 2
SHARE = N_Z * BITS
LOADS = P_OWN * SHARE
CHUNK = LOADS + 8
QUAD = 4
BACK = N_Y * P_OWN * BITS + QUAD
FIRST_Z = 10
FIRST_CHIP = 10
VMEM_LIMIT = 40 * 1024 * 1024


def iota(shape, axis):
    return lax.broadcasted_iota(jnp.int32, shape, axis)


def condense_kernel(
    ply_hbm,
    slot_hbm,
    inverse_hbm,
    coupling_hbm,
    stiffness_hbm,
    interior_hbm,
    boundary_hbm,
    sums,
    own_loads,
    twin_ref,
    ply_ref,
    slot_ref,
    inverse_buf,
    coupling_buf,
    stiffness_ref,
    interior_ref,
    boundary_ref,
    rows_ref,
    panels,
    extra,
    sems,
    small_sems,
):
    subs, inner_size, width = coupling_buf.shape
    plies = extra.shape[0]
    chips = twin_ref.shape[0]
    core = lax.rem(lax.axis_index("ply"), CORES)
    small = [
        pltpu.make_async_copy(source, target, small_sems.at[n])
        for n, (source, target) in enumerate(
            (
                (ply_hbm, ply_ref),
                (slot_hbm, slot_ref),
                (stiffness_hbm, stiffness_ref),
                (interior_hbm, interior_ref),
                (boundary_hbm, boundary_ref),
            )
        )
    ]
    def sub_copies(s):
        return (
            pltpu.make_async_copy(inverse_hbm.at[s], inverse_buf.at[s], sems.at[0, s]),
            pltpu.make_async_copy(coupling_hbm.at[s], coupling_buf.at[s], sems.at[1, s]),
        )

    for copy in (*sub_copies(0), *small, *sub_copies(1)):
        copy.start()
    sums[...] = jnp.zeros_like(sums)
    extra[...] = jnp.zeros_like(extra)
    same = iota((PR, PR), 0) == iota((PR, PR), 1)
    for copy in small:
        copy.wait()
    rows_ref[0:subs, 0:width] = stiffness_ref[...].astype(jnp.float32)
    rows_ref[8 : 8 + subs, 0:inner_size] = interior_ref[...].astype(jnp.float32)
    rows_ref[16 : 16 + subs, 0:width] = boundary_ref[...].astype(jnp.float32)

    def subregion(s, carry):
        for copy in sub_copies(s):
            copy.wait()

        @pl.when(s + 2 < subs)
        def _():
            for copy in sub_copies(s + 2):
                copy.start()

        stiffness = rows_ref[pl.ds(s, 1), 0:width]
        interior = rows_ref[pl.ds(8 + s, 1), 0:inner_size]
        boundary = rows_ref[pl.ds(16 + s, 1), 0:width]
        inverse = inverse_buf[s]
        coupling = coupling_buf[s]
        turned = coupling.T
        solved = jnp.sum(inverse.astype(jnp.float32) * interior, axis=1, keepdims=True)
        solved = solved.astype(jnp.bfloat16).astype(jnp.float32)
        inner = jnp.dot(inverse, coupling, preferred_element_type=jnp.float32)
        inner = inner.astype(jnp.bfloat16)
        carried = jnp.sum(coupling.astype(jnp.float32) * solved, axis=0, keepdims=True)
        condensed = (boundary - carried).astype(jnp.bfloat16).astype(jnp.float32)
        for k in range(NPS):
            columns = slice(k * PR, (k + 1) * PR)
            product = jnp.dot(
                turned[columns], inner[:, columns], preferred_element_type=jnp.float32
            )
            panels[columns, :] = jnp.where(same, stiffness[:, columns], 0.0) - product
        for k in range(NPS):
            item = s * NPS + k
            q = ply_ref[item]
            slot = slot_ref[item]
            mine = lax.rem(q, CORES) == core

            rows = pl.ds(pl.multiple_of(slot * SHARE, SHARE), SHARE)
            places = [
                lax.rem(y * (chips // N_Y) + q // CORES + chips - FIRST_CHIP, chips)
                for y in range(N_Y)
            ]
            parts = [
                jnp.concatenate(
                    [
                        panels[pl.ds(k * PR + y * BITS + bit, N_Z, stride=N_Y * BITS), :]
                        for bit in range(BITS)
                    ],
                    axis=0,
                )
                for y in range(N_Y)
            ]

            which = jnp.where(mine, 0, 1)
            held = [sums[which, at, rows, :] for at in places]
            for at, part, before in zip(places, parts, held):
                sums[which, at, rows, :] = before + part
            extra[q, pl.ds(slot, 1), :] = (
                extra[q, pl.ds(slot, 1), :] + condensed[:, k * PR : (k + 1) * PR]
            )
        return carry

    lax.fori_loop(0, subs, subregion, 0)
    twin_ref[:, 0:LOADS, :] = sums[1].astype(jnp.bfloat16)
    for me in range(CORES):

        @pl.when(core == me)
        def _():
            for q in range(plies):
                rows = extra[q]
                for y in range(N_Y):
                    turned = rows if y == 0 else pltpu.roll(rows, PR - BITS * y, 1)
                    at = (y * (chips // N_Y) + q // CORES - FIRST_CHIP) % chips
                    if q % CORES == me:
                        own_loads[at] = turned
                    else:
                        twin_ref[at, LOADS:CHUNK, :] = turned.astype(jnp.bfloat16)


def merge_kernel(sums, own_loads, other_ref, out_ref):
    total = sums[0] + other_ref[:, 0:LOADS, :].astype(jnp.float32)
    out_ref[:, 0:LOADS, :] = total.astype(jnp.bfloat16)
    loads = own_loads[...] + other_ref[:, LOADS:CHUNK, :].astype(jnp.float32)
    out_ref[:, LOADS:CHUNK, :] = loads.astype(jnp.bfloat16)


def combine_kernel(got_ref, out_ref, totals):
    chips = got_ref.shape[0]
    per_y = chips // N_Y
    sums = []
    for y in range(N_Y):
        messages = [got_ref[(y * per_y + x - FIRST_CHIP) % chips] for x in range(per_y)]
        total = messages[0].astype(jnp.float32)
        for message in messages[1:]:
            total = total + message.astype(jnp.float32)
        totals[y * CHUNK : (y + 1) * CHUNK, :] = total
        sums.append(total)
    loads = jnp.concatenate([t[LOADS : LOADS + P_OWN] for t in sums], axis=0)
    loads = jnp.concatenate([loads, jnp.zeros((PR - N_Y * P_OWN, PR), jnp.float32)], axis=0)
    loads = loads.T
    for z in range(N_Z):
        place = (z - FIRST_Z) % N_Z
        for y in range(N_Y):
            for bit in range(BITS):
                slots = totals[pl.ds(y * CHUNK + bit * N_Z + z, P_OWN, stride=SHARE), :]
                out_ref[place, y * BITS + bit] = slots.astype(jnp.bfloat16)
        step = N_Y * BITS
        out_ref[place, N_Y * BITS] = loads[z * step : z * step + QUAD].astype(jnp.bfloat16)


def place_kernel(target_ref, got_ref, blocks_ref, loads_ref, got_blocks, got_loads):
    patches = target_ref.shape[1]
    z_owners = N_Y * P_OWN
    target = lax.rem(target_ref[...] + (N_Z - FIRST_Z) * z_owners, N_Z * z_owners)
    rows = N_Y * P_OWN * BITS
    got_loads[...] = jnp.zeros_like(got_loads)
    for z in range(N_Z):
        for n in range(rows // QUAD):
            owner = z * z_owners + n // BITS * QUAD
            got_blocks[n % BITS, owner : owner + QUAD, :] = got_ref[z, n].astype(jnp.float32)
        got_loads[z * 8 : z * 8 + QUAD, :] = got_ref[z, rows // QUAD].astype(jnp.float32)
    loads = got_loads[...].astype(jnp.bfloat16)
    choose_owner = jnp.where(iota((patches, patches), 0) == target, 1.0, 0.0).astype(jnp.bfloat16)
    for bit in range(BITS):
        blocks_ref[0, bit] = lax.dot_general(
            choose_owner,
            got_blocks[bit].astype(jnp.bfloat16),
            (((0,), (0,)), ((), ())),
            preferred_element_type=jnp.float32,
        )
        wanted = (target // z_owners) * 8 + bit
        choose = jnp.where(iota((N_Z * 8, patches), 0) == wanted, 1.0, 0.0).astype(jnp.bfloat16)
        picked = lax.dot_general(
            loads, choose, (((0,), (0,)), ((), ())), preferred_element_type=jnp.float32
        )[0:z_owners]
        mine = iota(picked.shape, 0) == target % z_owners
        loads_ref[0, bit : bit + 1, :] = jnp.sum(
            jnp.where(mine, picked, 0.0), axis=0, keepdims=True
        )


def vmem():
    return pl.BlockSpec(memory_space=pltpu.VMEM)


def condense(*arguments):
    touch_slot, interior_inverse, coupling = arguments[1:4]
    subs, inner_size, width = coupling.shape
    plies = lax.axis_size("ply")
    chips = N_Y * plies // CORES
    return pl.pallas_call(
        condense_kernel,
        out_shape=(
            jax.ShapeDtypeStruct((CORES, chips, LOADS, PR), jnp.float32),
            jax.ShapeDtypeStruct((chips, CHUNK - LOADS, PR), jnp.float32),
            jax.ShapeDtypeStruct((chips, CHUNK, PR), jnp.bfloat16),
        ),
        in_specs=[pl.BlockSpec(memory_space=pltpu.HBM)] * len(arguments),
        out_specs=(vmem(),) * 3,
        scratch_shapes=[
            pltpu.SMEM(touch_slot.shape, jnp.int32),
            pltpu.SMEM(touch_slot.shape, jnp.int32),
            pltpu.VMEM(interior_inverse.shape, jnp.bfloat16),
            pltpu.VMEM(coupling.shape, jnp.bfloat16),
            pltpu.VMEM((subs, width), jnp.bfloat16),
            pltpu.VMEM((subs, inner_size), jnp.bfloat16),
            pltpu.VMEM((subs, width), jnp.bfloat16),
            pltpu.VMEM((24, inner_size), jnp.float32),
            pltpu.VMEM((width, PR), jnp.float32),
            pltpu.VMEM((plies, 8, PR), jnp.float32),
            pltpu.SemaphoreType.DMA((2, subs)),
            pltpu.SemaphoreType.DMA((5,)),
        ],
        compiler_params=pltpu.CompilerParams(vmem_limit_bytes=VMEM_LIMIT),
        name="condense",
    )(*(pltpu.with_memory_space_constraint(argument, pltpu.HBM) for argument in arguments))


def merge(sums, own_loads, other):
    return pl.pallas_call(
        merge_kernel,
        out_shape=jax.ShapeDtypeStruct(other.shape, other.dtype),
        in_specs=[vmem()] * 3,
        out_specs=vmem(),
        compiler_params=pltpu.CompilerParams(vmem_limit_bytes=VMEM_LIMIT),
        name="merge",
    )(sums, own_loads, other)


def combine(got):
    return pl.pallas_call(
        combine_kernel,
        out_shape=jax.ShapeDtypeStruct((N_Z, BACK // QUAD, QUAD, PR), jnp.bfloat16),
        in_specs=[vmem()],
        out_specs=vmem(),
        scratch_shapes=[pltpu.VMEM((N_Y * CHUNK, PR), jnp.float32)],
        compiler_params=pltpu.CompilerParams(vmem_limit_bytes=VMEM_LIMIT),
        name="combine",
    )(got)


def place(target, got):
    patches = target.shape[1]
    return pl.pallas_call(
        place_kernel,
        out_shape=(
            jax.ShapeDtypeStruct((1, BITS, patches, PR), jnp.float32),
            jax.ShapeDtypeStruct((1, BITS, patches), jnp.float32),
        ),
        in_specs=[vmem(), vmem()],
        out_specs=(vmem(), vmem()),
        scratch_shapes=[
            pltpu.VMEM((BITS, patches, PR), jnp.float32),
            pltpu.VMEM((N_Z * 8, PR), jnp.float32),
        ],
        compiler_params=pltpu.CompilerParams(vmem_limit_bytes=VMEM_LIMIT),
        name="place",
    )(target, got)


def on_device(
    interior_inverse,
    coupling,
    boundary_stiffness,
    interior_load,
    boundary_load,
    touch_ply,
    touch_slot,
    source_position,
):
    sums, own_loads, twin = condense(
        touch_ply.reshape(-1),
        touch_slot,
        interior_inverse,
        coupling,
        boundary_stiffness,
        interior_load,
        boundary_load,
    )
    plies = lax.axis_size("ply")
    other = lax.ppermute(twin, "ply", [(q, q ^ 1) for q in range(plies)])
    chips = N_Y * plies // CORES
    got = lax.all_to_all(
        merge(sums, own_loads, other),
        ("wide", "ply"),
        split_axis=0,
        concat_axis=0,
        tiled=True,
        axis_index_groups=[
            [(z * chips + (i + FIRST_CHIP) % chips) * CORES + core for i in range(chips)]
            for z in range(N_Z)
            for core in range(CORES)
        ],
    )
    got = lax.all_to_all(
        combine(got),
        "wide",
        split_axis=0,
        concat_axis=0,
        tiled=True,
        axis_index_groups=[
            [(i + FIRST_Z) % N_Z * N_Y + y for i in range(N_Z)] for y in range(N_Y)
        ],
    )
    return place(source_position, got)


def solution(mesh):
    return jax.shard_map(
        on_device,
        mesh=mesh,
        in_specs=(
            P(("wide", "ply"), None, None),
            P(("wide", "ply"), None, None),
            P(("wide", "ply"), None),
            P(("wide", "ply"), None),
            P(("wide", "ply"), None),
            P(("wide", "ply"), None),
            P(("wide", "ply")),
            P("ply", None),
        ),
        out_specs=(P("ply", "wide", None, None), P("ply", "wide", None)),
        check_vma=False,
    )
```

```python
import jax
import jax.numpy as jnp
from jax import lax
from jax.experimental import pallas as pl
from jax.experimental.pallas import tpu as pltpu
from jax.sharding import PartitionSpec as P

PR = 128
NPS = 4
P_OWN = 4
CAP = 3
N_Z = 16
N_Y = 4
BITS = 2
SHARE = N_Z * BITS
CHUNK = CAP * SHARE + 8
CODE_ROW = CAP
LOADS = SHARE * P_OWN
QUAD = 4
BACK = N_Y * P_OWN * BITS + QUAD
Z_ORDER = (11, 6, 8, 15, 12, 3, 10, 5, 2, 14, 0, 4, 7, 1, 9, 13)
PLANE_ORDER = (
    21, 9, 24, 14, 10, 28, 1, 5, 3, 22, 23, 13, 12, 29, 16, 27,
    6, 31, 8, 25, 0, 26, 2, 30, 20, 15, 19, 11, 4, 17, 18, 7,
)
VMEM_LIMIT = 40 * 1024 * 1024


def iota(shape, axis):
    return lax.broadcasted_iota(jnp.int32, shape, axis)


def condense_kernel(
    ply_hbm,
    slot_hbm,
    inverse_hbm,
    coupling_hbm,
    stiffness_hbm,
    interior_hbm,
    boundary_hbm,
    out_ref,
    ply_ref,
    slot_ref,
    inverse_buf,
    coupling_buf,
    stiffness_ref,
    interior_ref,
    boundary_ref,
    rows_ref,
    panels,
    extra,
    count,
    places,
    sems,
    small_sems,
):
    subs, inner_size, width = coupling_buf.shape
    plies = extra.shape[0]
    small = [
        pltpu.make_async_copy(source, target, small_sems.at[n])
        for n, (source, target) in enumerate(
            (
                (ply_hbm, ply_ref),
                (slot_hbm, slot_ref),
                (stiffness_hbm, stiffness_ref),
                (interior_hbm, interior_ref),
                (boundary_hbm, boundary_ref),
            )
        )
    ]
    def sub_copies(s):
        return (
            pltpu.make_async_copy(inverse_hbm.at[s], inverse_buf.at[s], sems.at[0, s]),
            pltpu.make_async_copy(coupling_hbm.at[s], coupling_buf.at[s], sems.at[1, s]),
        )

    for copy in (*sub_copies(0), *small, *sub_copies(1)):
        copy.start()
    out_ref[...] = jnp.zeros_like(out_ref)
    extra[...] = jnp.where(iota(extra.shape, 1) == CODE_ROW, -1.0, 0.0)
    for q in range(plies):
        count[q] = 0
    for place, device in enumerate(PLANE_ORDER):
        places[device] = place
    lane = iota((1, PR), 1)
    row_code = (lane % N_Z) * (BITS * P_OWN) + ((lane // N_Z) % BITS) * P_OWN
    row_item = lane // SHARE
    same = iota((PR, PR), 0) == iota((PR, PR), 1)
    for copy in small:
        copy.wait()
    rows_ref[0:subs, 0:width] = stiffness_ref[...].astype(jnp.float32)
    rows_ref[8 : 8 + subs, 0:inner_size] = interior_ref[...].astype(jnp.float32)
    rows_ref[16 : 16 + subs, 0:width] = boundary_ref[...].astype(jnp.float32)

    def subregion(s):
        for copy in sub_copies(s):
            copy.wait()

        if s + 2 < subs:
            for copy in sub_copies(s + 2):
                copy.start()

        stiffness = rows_ref[pl.ds(s, 1), 0:width]
        interior = rows_ref[pl.ds(8 + s, 1), 0:inner_size]
        boundary = rows_ref[pl.ds(16 + s, 1), 0:width]
        inverse = inverse_buf[s]
        coupling = coupling_buf[s]
        turned = coupling.T
        solved = jnp.sum(inverse.astype(jnp.float32) * interior, axis=1, keepdims=True)
        solved = solved.astype(jnp.bfloat16).astype(jnp.float32)
        inner = jnp.dot(inverse, coupling, preferred_element_type=jnp.float32)
        inner = inner.astype(jnp.bfloat16)
        carried = jnp.sum(coupling.astype(jnp.float32) * solved, axis=0, keepdims=True)
        condensed = (boundary - carried).astype(jnp.bfloat16).astype(jnp.float32)
        for k in range(NPS):
            columns = slice(k * PR, (k + 1) * PR)
            product = jnp.dot(
                turned[columns], inner[:, columns], preferred_element_type=jnp.float32
            )
            panels[s, columns, :] = jnp.where(same, stiffness[:, columns], 0.0) - product
        for k in range(NPS):
            item = s * NPS + k
            q = ply_ref[item]
            slot = slot_ref[item]
            rank = count[q]
            count[q] = rank + 1
            for y in range(N_Y):
                part = [
                    panels[s, pl.ds(k * PR + y * BITS + bit, N_Z, stride=N_Y * BITS), :]
                    for bit in range(BITS)
                ]
                place = places[y * plies + q]
                out_ref[place, pl.ds(pl.multiple_of(rank * SHARE, SHARE), SHARE), :] = (
                    jnp.concatenate(part, axis=0).astype(jnp.bfloat16)
                )
            extra[q, pl.ds(rank, 1), :] = condensed[:, k * PR : (k + 1) * PR]
            codes = extra[q, CODE_ROW : CODE_ROW + 1, :]
            codes = jnp.where(row_item == rank, (row_code + slot).astype(jnp.float32), codes)
            codes = jnp.where(
                lane == CAP * SHARE + rank, (LOADS + slot).astype(jnp.float32), codes
            )
            extra[q, CODE_ROW : CODE_ROW + 1, :] = codes
    for s in range(subs):
        subregion(s)
    is_code = iota((8, PR), 0) == CODE_ROW
    for q in range(plies):
        rows = extra[q]
        for y in range(N_Y):
            turned = rows if y == 0 else pltpu.roll(rows, PR - BITS * y, 1)
            place = PLANE_ORDER.index(y * plies + q)
            out_ref[place, CAP * SHARE : CHUNK, :] = jnp.where(
                is_code, rows, turned
            ).astype(jnp.bfloat16)


def combine_kernel(got_ref, out_ref):
    plies = got_ref.shape[0] // N_Y
    sum_rows = iota((LOADS + 8, plies * PR), 0).astype(jnp.float32)
    sums = []
    for y in range(N_Y):
        messages = [got_ref[PLANE_ORDER.index(y * plies + q)] for q in range(plies)]
        codes = jnp.concatenate(
            [
                m[CAP * SHARE : CHUNK].astype(jnp.float32)[CODE_ROW : CODE_ROW + 1]
                for m in messages
            ],
            axis=1,
        )
        choose = (sum_rows == codes).astype(jnp.bfloat16)
        pad = jnp.zeros((PR - CHUNK, PR), jnp.bfloat16)
        rows = jnp.concatenate([v for m in messages for v in (m, pad)], axis=0)
        sums.append(jnp.dot(choose, rows, preferred_element_type=jnp.float32))
    loads = jnp.concatenate([t[LOADS : LOADS + P_OWN] for t in sums], axis=0)
    loads = jnp.concatenate([loads, jnp.zeros((PR - N_Y * P_OWN, PR), jnp.float32)], axis=0)
    loads = loads.T
    step = BITS * P_OWN
    for z in range(N_Z):
        place = Z_ORDER.index(z)
        rows = [t[z * step : (z + 1) * step] for t in sums] + [loads[z * step : z * step + QUAD]]
        for n, row in enumerate(rows):
            for half in range(row.shape[0] // QUAD):
                out_ref[place, n * (step // QUAD) + half] = row[
                    half * QUAD : (half + 1) * QUAD
                ].astype(jnp.bfloat16)


def place_kernel(target_ref, got_ref, blocks_ref, loads_ref, got_blocks, got_loads):
    patches = target_ref.shape[1]
    z_owners = N_Y * P_OWN
    target = target_ref[...]
    first = jnp.zeros_like(target)
    for place, z in enumerate(Z_ORDER):
        first = jnp.where(target // z_owners == z, place * z_owners, first)
    target = first + target % z_owners
    rows = N_Y * P_OWN * BITS
    got_loads[...] = jnp.zeros_like(got_loads)
    for z in range(N_Z):
        for n in range(rows // QUAD):
            owner = z * z_owners + n // BITS * QUAD
            got_blocks[n % BITS, owner : owner + QUAD, :] = got_ref[z, n].astype(jnp.float32)
        got_loads[z * 8 : z * 8 + QUAD, :] = got_ref[z, rows // QUAD].astype(jnp.float32)
    loads = got_loads[...].astype(jnp.bfloat16)
    choose_owner = jnp.where(iota((patches, patches), 0) == target, 1.0, 0.0).astype(jnp.bfloat16)
    for bit in range(BITS):
        blocks_ref[0, bit] = lax.dot_general(
            choose_owner,
            got_blocks[bit].astype(jnp.bfloat16),
            (((0,), (0,)), ((), ())),
            preferred_element_type=jnp.float32,
        )
        wanted = (target // z_owners) * 8 + bit
        choose = jnp.where(iota((N_Z * 8, patches), 0) == wanted, 1.0, 0.0).astype(jnp.bfloat16)
        picked = lax.dot_general(
            loads, choose, (((0,), (0,)), ((), ())), preferred_element_type=jnp.float32
        )[0:z_owners]
        mine = iota(picked.shape, 0) == target % z_owners
        loads_ref[0, bit : bit + 1, :] = jnp.sum(
            jnp.where(mine, picked, 0.0), axis=0, keepdims=True
        )


def vmem():
    return pl.BlockSpec(memory_space=pltpu.VMEM)


def condense(*arguments):
    touch_slot, interior_inverse, coupling = arguments[1:4]
    subs, inner_size, width = coupling.shape
    plies = lax.axis_size("ply")
    return pl.pallas_call(
        condense_kernel,
        out_shape=jax.ShapeDtypeStruct((N_Y * plies, CHUNK, PR), jnp.bfloat16),
        in_specs=[pl.BlockSpec(memory_space=pltpu.HBM)] * len(arguments),
        out_specs=vmem(),
        scratch_shapes=[
            pltpu.SMEM(touch_slot.shape, jnp.int32),
            pltpu.SMEM(touch_slot.shape, jnp.int32),
            pltpu.VMEM(interior_inverse.shape, jnp.bfloat16),
            pltpu.VMEM(coupling.shape, jnp.bfloat16),
            pltpu.VMEM((subs, width), jnp.bfloat16),
            pltpu.VMEM((subs, inner_size), jnp.bfloat16),
            pltpu.VMEM((subs, width), jnp.bfloat16),
            pltpu.VMEM((24, inner_size), jnp.float32),
            pltpu.VMEM((subs, width, PR), jnp.float32),
            pltpu.VMEM((plies, 8, PR), jnp.float32),
            pltpu.SMEM((plies,), jnp.int32),
            pltpu.SMEM((N_Y * plies,), jnp.int32),
            pltpu.SemaphoreType.DMA((2, subs)),
            pltpu.SemaphoreType.DMA((5,)),
        ],
        compiler_params=pltpu.CompilerParams(vmem_limit_bytes=VMEM_LIMIT),
        name="condense",
    )(*(pltpu.with_memory_space_constraint(argument, pltpu.HBM) for argument in arguments))


def combine(got):
    return pl.pallas_call(
        combine_kernel,
        out_shape=jax.ShapeDtypeStruct((N_Z, BACK // QUAD, QUAD, PR), jnp.bfloat16),
        in_specs=[vmem()],
        out_specs=vmem(),
        compiler_params=pltpu.CompilerParams(vmem_limit_bytes=VMEM_LIMIT),
        name="combine",
    )(got)


def place(target, got):
    patches = target.shape[1]
    return pl.pallas_call(
        place_kernel,
        out_shape=(
            jax.ShapeDtypeStruct((1, BITS, patches, PR), jnp.float32),
            jax.ShapeDtypeStruct((1, BITS, patches), jnp.float32),
        ),
        in_specs=[vmem(), vmem()],
        out_specs=(vmem(), vmem()),
        scratch_shapes=[
            pltpu.VMEM((BITS, patches, PR), jnp.float32),
            pltpu.VMEM((N_Z * 8, PR), jnp.float32),
        ],
        compiler_params=pltpu.CompilerParams(vmem_limit_bytes=VMEM_LIMIT),
        name="place",
    )(target, got)


def on_device(
    interior_inverse,
    coupling,
    boundary_stiffness,
    interior_load,
    boundary_load,
    touch_ply,
    touch_slot,
    source_position,
):
    send = condense(
        touch_ply.reshape(-1),
        touch_slot,
        interior_inverse,
        coupling,
        boundary_stiffness,
        interior_load,
        boundary_load,
    )
    plane = N_Y * lax.axis_size("ply")
    got = lax.all_to_all(
        send,
        ("wide", "ply"),
        split_axis=0,
        concat_axis=0,
        tiled=True,
        axis_index_groups=[[z * plane + i for i in PLANE_ORDER] for z in range(N_Z)],
    )
    got = lax.all_to_all(
        combine(got),
        "wide",
        split_axis=0,
        concat_axis=0,
        tiled=True,
        axis_index_groups=[[z * N_Y + y for z in Z_ORDER] for y in range(N_Y)],
    )
    return place(source_position, got)


def solution(mesh):
    return jax.shard_map(
        on_device,
        mesh=mesh,
        in_specs=(
            P(("wide", "ply"), None, None),
            P(("wide", "ply"), None, None),
            P(("wide", "ply"), None),
            P(("wide", "ply"), None),
            P(("wide", "ply"), None),
            P(("wide", "ply"), None),
            P(("wide", "ply")),
            P("ply", None),
        ),
        out_specs=(P("ply", "wide", None, None), P("ply", "wide", None)),
        check_vma=False,
    )
```

```python
import jax
import jax.numpy as jnp
from jax import lax
from jax.experimental import pallas as pl
from jax.experimental.pallas import tpu as pltpu
from jax.sharding import PartitionSpec as P

PR = 128
NPS = 4
P_OWN = 4
N_Z = 16
N_Y = 4
CORES = 2
BITS = 2
SHARE = N_Z * BITS
LOADS = P_OWN * SHARE
CHUNK = LOADS + 8
QUAD = 4
BACK = N_Y * P_OWN * BITS + QUAD
Z_ORDER = (11, 6, 8, 15, 12, 3, 10, 5, 2, 14, 0, 4, 7, 1, 9, 13)
CHIP_ORDER = (10, 3, 13, 15, 7, 12, 4, 14, 9, 8, 1, 0, 11, 6, 2, 5)
VMEM_LIMIT = 40 * 1024 * 1024


def iota(shape, axis):
    return lax.broadcasted_iota(jnp.int32, shape, axis)


def condense_kernel(
    ply_hbm,
    slot_hbm,
    inverse_hbm,
    coupling_hbm,
    stiffness_hbm,
    interior_hbm,
    boundary_hbm,
    sums,
    own_loads,
    twin_ref,
    ply_ref,
    slot_ref,
    inverse_buf,
    coupling_buf,
    stiffness_ref,
    interior_ref,
    boundary_ref,
    rows_ref,
    panels,
    extra,
    table,
    sems,
    small_sems,
):
    subs, inner_size, width = coupling_buf.shape
    plies = extra.shape[0]
    chips = twin_ref.shape[0]
    core = lax.rem(lax.axis_index("ply"), CORES)
    small = [
        pltpu.make_async_copy(source, target, small_sems.at[n])
        for n, (source, target) in enumerate(
            (
                (ply_hbm, ply_ref),
                (slot_hbm, slot_ref),
                (stiffness_hbm, stiffness_ref),
                (interior_hbm, interior_ref),
                (boundary_hbm, boundary_ref),
            )
        )
    ]
    def sub_copies(s):
        return (
            pltpu.make_async_copy(inverse_hbm.at[s], inverse_buf.at[s], sems.at[0, s]),
            pltpu.make_async_copy(coupling_hbm.at[s], coupling_buf.at[s], sems.at[1, s]),
        )

    for copy in (*sub_copies(0), *small, *sub_copies(1)):
        copy.start()
    sums[...] = jnp.zeros_like(sums)
    extra[...] = jnp.zeros_like(extra)
    for place, chip in enumerate(CHIP_ORDER):
        table[chip] = place
    same = iota((PR, PR), 0) == iota((PR, PR), 1)
    for copy in small:
        copy.wait()
    rows_ref[0:subs, 0:width] = stiffness_ref[...].astype(jnp.float32)
    rows_ref[8 : 8 + subs, 0:inner_size] = interior_ref[...].astype(jnp.float32)
    rows_ref[16 : 16 + subs, 0:width] = boundary_ref[...].astype(jnp.float32)

    def subregion(s):
        for copy in sub_copies(s):
            copy.wait()

        if s + 2 < subs:
            for copy in sub_copies(s + 2):
                copy.start()

        stiffness = rows_ref[pl.ds(s, 1), 0:width]
        interior = rows_ref[pl.ds(8 + s, 1), 0:inner_size]
        boundary = rows_ref[pl.ds(16 + s, 1), 0:width]
        inverse = inverse_buf[s]
        coupling = coupling_buf[s]
        turned = coupling.T
        solved = jnp.sum(inverse.astype(jnp.float32) * interior, axis=1, keepdims=True)
        solved = solved.astype(jnp.bfloat16).astype(jnp.float32)
        inner = jnp.dot(inverse, coupling, preferred_element_type=jnp.float32)
        inner = inner.astype(jnp.bfloat16)
        carried = jnp.sum(coupling.astype(jnp.float32) * solved, axis=0, keepdims=True)
        condensed = (boundary - carried).astype(jnp.bfloat16).astype(jnp.float32)
        for k in range(NPS):
            columns = slice(k * PR, (k + 1) * PR)
            product = jnp.dot(
                turned[columns], inner[:, columns], preferred_element_type=jnp.float32
            )
            panels[s, columns, :] = jnp.where(same, stiffness[:, columns], 0.0) - product
        for k in range(NPS):
            item = s * NPS + k
            q = ply_ref[item]
            slot = slot_ref[item]
            mine = lax.rem(q, CORES) == core

            rows = pl.ds(pl.multiple_of(slot * SHARE, SHARE), SHARE)
            places = [
                table[y * (chips // N_Y) + q // CORES]
                for y in range(N_Y)
            ]
            parts = [
                jnp.concatenate(
                    [
                        panels[s, pl.ds(k * PR + y * BITS + bit, N_Z, stride=N_Y * BITS), :]
                        for bit in range(BITS)
                    ],
                    axis=0,
                )
                for y in range(N_Y)
            ]

            which = jnp.where(mine, 0, 1)
            held = [sums[which, at, rows, :] for at in places]
            for at, part, before in zip(places, parts, held):
                sums[which, at, rows, :] = before + part
            extra[q, pl.ds(slot, 1), :] = (
                extra[q, pl.ds(slot, 1), :] + condensed[:, k * PR : (k + 1) * PR]
            )
    for s in range(subs):
        subregion(s)
    twin_ref[:, 0:LOADS, :] = sums[1].astype(jnp.bfloat16)
    for me in range(CORES):

        @pl.when(core == me)
        def _():
            for q in range(plies):
                rows = extra[q]
                for y in range(N_Y):
                    turned = rows if y == 0 else pltpu.roll(rows, PR - BITS * y, 1)
                    at = CHIP_ORDER.index(y * (chips // N_Y) + q // CORES)
                    if q % CORES == me:
                        own_loads[at] = turned
                    else:
                        twin_ref[at, LOADS:CHUNK, :] = turned.astype(jnp.bfloat16)


def merge_kernel(sums, own_loads, other_ref, out_ref):
    total = sums[0] + other_ref[:, 0:LOADS, :].astype(jnp.float32)
    out_ref[:, 0:LOADS, :] = total.astype(jnp.bfloat16)
    loads = own_loads[...] + other_ref[:, LOADS:CHUNK, :].astype(jnp.float32)
    out_ref[:, LOADS:CHUNK, :] = loads.astype(jnp.bfloat16)


def combine_kernel(got_ref, out_ref, totals):
    chips = got_ref.shape[0]
    per_y = chips // N_Y
    sums = []
    for y in range(N_Y):
        messages = [got_ref[CHIP_ORDER.index(y * per_y + x)] for x in range(per_y)]
        total = messages[0].astype(jnp.float32)
        for message in messages[1:]:
            total = total + message.astype(jnp.float32)
        totals[y * CHUNK : (y + 1) * CHUNK, :] = total
        sums.append(total)
    loads = jnp.concatenate([t[LOADS : LOADS + P_OWN] for t in sums], axis=0)
    loads = jnp.concatenate([loads, jnp.zeros((PR - N_Y * P_OWN, PR), jnp.float32)], axis=0)
    loads = loads.T
    for z in range(N_Z):
        place = Z_ORDER.index(z)
        for y in range(N_Y):
            for bit in range(BITS):
                slots = totals[pl.ds(y * CHUNK + bit * N_Z + z, P_OWN, stride=SHARE), :]
                out_ref[place, y * BITS + bit] = slots.astype(jnp.bfloat16)
        step = N_Y * BITS
        out_ref[place, N_Y * BITS] = loads[z * step : z * step + QUAD].astype(jnp.bfloat16)


def place_kernel(target_ref, got_ref, blocks_ref, loads_ref, got_blocks, got_loads):
    patches = target_ref.shape[1]
    z_owners = N_Y * P_OWN
    target = target_ref[...]
    first = jnp.zeros_like(target)
    for place, z in enumerate(Z_ORDER):
        first = jnp.where(target // z_owners == z, place * z_owners, first)
    target = first + target % z_owners
    rows = N_Y * P_OWN * BITS
    got_loads[...] = jnp.zeros_like(got_loads)
    for z in range(N_Z):
        for n in range(rows // QUAD):
            owner = z * z_owners + n // BITS * QUAD
            got_blocks[n % BITS, owner : owner + QUAD, :] = got_ref[z, n].astype(jnp.float32)
        got_loads[z * 8 : z * 8 + QUAD, :] = got_ref[z, rows // QUAD].astype(jnp.float32)
    loads = got_loads[...].astype(jnp.bfloat16)
    choose_owner = jnp.where(iota((patches, patches), 0) == target, 1.0, 0.0).astype(jnp.bfloat16)
    for bit in range(BITS):
        blocks_ref[0, bit] = lax.dot_general(
            choose_owner,
            got_blocks[bit].astype(jnp.bfloat16),
            (((0,), (0,)), ((), ())),
            preferred_element_type=jnp.float32,
        )
        wanted = (target // z_owners) * 8 + bit
        choose = jnp.where(iota((N_Z * 8, patches), 0) == wanted, 1.0, 0.0).astype(jnp.bfloat16)
        picked = lax.dot_general(
            loads, choose, (((0,), (0,)), ((), ())), preferred_element_type=jnp.float32
        )[0:z_owners]
        mine = iota(picked.shape, 0) == target % z_owners
        loads_ref[0, bit : bit + 1, :] = jnp.sum(
            jnp.where(mine, picked, 0.0), axis=0, keepdims=True
        )


def vmem():
    return pl.BlockSpec(memory_space=pltpu.VMEM)


def condense(*arguments):
    touch_slot, interior_inverse, coupling = arguments[1:4]
    subs, inner_size, width = coupling.shape
    plies = lax.axis_size("ply")
    chips = N_Y * plies // CORES
    return pl.pallas_call(
        condense_kernel,
        out_shape=(
            jax.ShapeDtypeStruct((CORES, chips, LOADS, PR), jnp.float32),
            jax.ShapeDtypeStruct((chips, CHUNK - LOADS, PR), jnp.float32),
            jax.ShapeDtypeStruct((chips, CHUNK, PR), jnp.bfloat16),
        ),
        in_specs=[pl.BlockSpec(memory_space=pltpu.HBM)] * len(arguments),
        out_specs=(vmem(),) * 3,
        scratch_shapes=[
            pltpu.SMEM(touch_slot.shape, jnp.int32),
            pltpu.SMEM(touch_slot.shape, jnp.int32),
            pltpu.VMEM(interior_inverse.shape, jnp.bfloat16),
            pltpu.VMEM(coupling.shape, jnp.bfloat16),
            pltpu.VMEM((subs, width), jnp.bfloat16),
            pltpu.VMEM((subs, inner_size), jnp.bfloat16),
            pltpu.VMEM((subs, width), jnp.bfloat16),
            pltpu.VMEM((24, inner_size), jnp.float32),
            pltpu.VMEM((subs, width, PR), jnp.float32),
            pltpu.VMEM((plies, 8, PR), jnp.float32),
            pltpu.SMEM((chips,), jnp.int32),
            pltpu.SemaphoreType.DMA((2, subs)),
            pltpu.SemaphoreType.DMA((5,)),
        ],
        compiler_params=pltpu.CompilerParams(vmem_limit_bytes=VMEM_LIMIT),
        name="condense",
    )(*(pltpu.with_memory_space_constraint(argument, pltpu.HBM) for argument in arguments))


def merge(sums, own_loads, other):
    return pl.pallas_call(
        merge_kernel,
        out_shape=jax.ShapeDtypeStruct(other.shape, other.dtype),
        in_specs=[vmem()] * 3,
        out_specs=vmem(),
        compiler_params=pltpu.CompilerParams(vmem_limit_bytes=VMEM_LIMIT),
        name="merge",
    )(sums, own_loads, other)


def combine(got):
    return pl.pallas_call(
        combine_kernel,
        out_shape=jax.ShapeDtypeStruct((N_Z, BACK // QUAD, QUAD, PR), jnp.bfloat16),
        in_specs=[vmem()],
        out_specs=vmem(),
        scratch_shapes=[pltpu.VMEM((N_Y * CHUNK, PR), jnp.float32)],
        compiler_params=pltpu.CompilerParams(vmem_limit_bytes=VMEM_LIMIT),
        name="combine",
    )(got)


def place(target, got):
    patches = target.shape[1]
    return pl.pallas_call(
        place_kernel,
        out_shape=(
            jax.ShapeDtypeStruct((1, BITS, patches, PR), jnp.float32),
            jax.ShapeDtypeStruct((1, BITS, patches), jnp.float32),
        ),
        in_specs=[vmem(), vmem()],
        out_specs=(vmem(), vmem()),
        scratch_shapes=[
            pltpu.VMEM((BITS, patches, PR), jnp.float32),
            pltpu.VMEM((N_Z * 8, PR), jnp.float32),
        ],
        compiler_params=pltpu.CompilerParams(vmem_limit_bytes=VMEM_LIMIT),
        name="place",
    )(target, got)


def on_device(
    interior_inverse,
    coupling,
    boundary_stiffness,
    interior_load,
    boundary_load,
    touch_ply,
    touch_slot,
    source_position,
):
    sums, own_loads, twin = condense(
        touch_ply.reshape(-1),
        touch_slot,
        interior_inverse,
        coupling,
        boundary_stiffness,
        interior_load,
        boundary_load,
    )
    plies = lax.axis_size("ply")
    other = lax.ppermute(twin, "ply", [(q, q ^ 1) for q in range(plies)])
    chips = N_Y * plies // CORES
    got = lax.all_to_all(
        merge(sums, own_loads, other),
        ("wide", "ply"),
        split_axis=0,
        concat_axis=0,
        tiled=True,
        axis_index_groups=[
            [(z * chips + chip) * CORES + core for chip in CHIP_ORDER]
            for z in range(N_Z)
            for core in range(CORES)
        ],
    )
    got = lax.all_to_all(
        combine(got),
        "wide",
        split_axis=0,
        concat_axis=0,
        tiled=True,
        axis_index_groups=[[z * N_Y + y for z in Z_ORDER] for y in range(N_Y)],
    )
    return place(source_position, got)


def solution(mesh):
    return jax.shard_map(
        on_device,
        mesh=mesh,
        in_specs=(
            P(("wide", "ply"), None, None),
            P(("wide", "ply"), None, None),
            P(("wide", "ply"), None),
            P(("wide", "ply"), None),
            P(("wide", "ply"), None),
            P(("wide", "ply"), None),
            P(("wide", "ply")),
            P("ply", None),
        ),
        out_specs=(P("ply", "wide", None, None), P("ply", "wide", None)),
        check_vma=False,
    )
```
